32 devices in a mesh: seq: 16 (over z, y, x), tp: 2 (over core).
Axes of the slice: x: 2, y: 2, z: 4, core: 2. Of those that a mesh axis runs over, the one named last changes fastest.
Arguments:
- mamba_x: bfloat16 [1024, 8192], P('seq', 'tp'), may hold values from -6 to 6
- gate_z: bfloat16 [1024, 8192], P('seq', 'tp'), may hold values from -6 to 6
- b_in: bfloat16 [1024, 1024], P('seq', 'tp'), may hold values from -1.25 to 1.25
- c_in: bfloat16 [1024, 1024], P('seq', 'tp'), may hold values from -1.25 to 1.25
- dt_raw: float32 [128, 1024], P('tp', 'seq'), may hold values from -2 to 6144
- a_log: float32 [128], P('tp'), may hold values from -14 to -3
- skip_d: float32 [128], P('tp'), may hold values from 0.5 to 1.5
- norm_gain: float32 [8192], P('tp'), may hold values from 0.5 to 1.5
- value_weight: bfloat16 [8192, 1024], P('tp'), may hold values from -0.09375 to 0.09375
- queries: bfloat16 [1024, 4096], P('seq', 'tp'), may hold values from -18 to 18
- keys: bfloat16 [1024, 1024], P('seq', 'tp'), may hold values from -4.5 to 4.5
Outputs:
- mamba_out: bfloat16 [1024, 8192], P('seq', 'tp')
- attention: bfloat16 [1024, 4096], P('seq', 'tp')
The draws below stay inside these ranges and needn't reach their ends.
All inputs are finite; a program needn't handle non-finite values.
Results may differ from the reference program's by a relative error of at most 0.02.
Values may be sent and summed in bfloat16 or wider, within the bound.
A program may use at most 128 MiB of HBM per device.

```python
import math
import jax
import jax.numpy as jnp
from jax import lax

MHEADS = 128
MHEAD_DIM = 64
STATE = 128
NGROUPS = 8
QHEADS = 32
KVHEADS = 8
HEAD_DIM = 128
TOK_DEV = 64
INNER = 8192
SPAN_OF_INPUT = 1024
N_SEQ = 16


def decay_plan(key):
    base_key = jax.random.fold_in(key, 7)
    concurrent_tracks = jax.random.split(base_key, 6)
    fast_cut = 5
    fast_heads = jax.random.randint(concurrent_tracks[0], (MHEADS,), 0, 10) < fast_cut
    slow_rate = jnp.exp(jax.random.uniform(concurrent_tracks[1], (MHEADS,), jnp.float32, math.log(0.1), math.log(0.35))) / SPAN_OF_INPUT
    fast_rate = jax.random.uniform(concurrent_tracks[2], (MHEADS,), jnp.float32, 0.02, 0.034)
    per_channel_fading = jnp.where(fast_heads, fast_rate, slow_rate)
    roughness = jnp.exp(jax.random.uniform(concurrent_tracks[3], (MHEADS, SPAN_OF_INPUT), jnp.float32, math.log(0.5), math.log(2.0)))
    block_total = SPAN_OF_INPUT // TOK_DEV
    levels = jnp.exp(jax.random.uniform(concurrent_tracks[4], (MHEADS, block_total), jnp.float32, math.log(0.5), math.log(2.0)))
    discrete_increment = roughness * jnp.repeat(levels, TOK_DEV, axis=1)
    pulse_offset_index = jax.random.randint(concurrent_tracks[5], (3,), 0, SPAN_OF_INPUT)
    surviving_fraction = jax.random.uniform(jax.random.fold_in(base_key, 9), (3, MHEADS), jnp.float32, 0.55, 0.8)
    element_indices = jnp.arange(SPAN_OF_INPUT)
    for pulse_extent in range(3):
        flagged_entries = element_indices[None, :] == pulse_offset_index[pulse_extent]
        pulse_spacing = (-jnp.log(surviving_fraction[pulse_extent]) / per_channel_fading)[:, None]
        discrete_increment = jnp.where(flagged_entries, pulse_spacing, discrete_increment)
    return (per_channel_fading, discrete_increment)


def draw_a_log(key, part):
    per_channel_fading, discrete_increment = decay_plan(key)
    return jnp.log(per_channel_fading)


def draw_dt_raw(key, part):
    per_channel_fading, discrete_increment = decay_plan(key)
    return discrete_increment + jnp.log(-jnp.expm1(-discrete_increment))


def attention_pair(key):
    base_key = jax.random.fold_in(key, 3)
    concurrent_tracks = jax.random.split(base_key, 2)
    key_shape = (SPAN_OF_INPUT, KVHEADS * HEAD_DIM)
    query_shape = (SPAN_OF_INPUT, QHEADS * HEAD_DIM)
    key_rows = jnp.clip(jax.random.normal(concurrent_tracks[0], key_shape, jnp.float32), -4.5, 4.5)
    query_rows = 2.0 * jnp.clip(jax.random.normal(concurrent_tracks[1], query_shape, jnp.float32), -4.5, 4.5)
    return (query_rows, key_rows)


def draw_queries(key, part):
    query_rows, key_rows = attention_pair(key)
    return query_rows.astype(jnp.bfloat16)


def draw_keys(key, part):
    query_rows, key_rows = attention_pair(key)
    return key_rows.astype(jnp.bfloat16)


def raised(drawn, stream_key, source, target, parts, factor):
    def block_of(dim):
        return (jnp.arange(drawn.shape[dim]) // (drawn.shape[dim] // parts)).reshape((-1,) + (1,) * (drawn.ndim - 1 - dim))

    near = jax.random.permutation(stream_key, parts)[block_of(target)]
    second = (block_of(target) + parts // 2) % parts
    return jnp.where((block_of(source) == near) | (block_of(source) == second), factor * drawn, drawn)


def level_of(own_key, dims, cuts, least, largest):
    gain, own = 1.0, jax.random.fold_in(own_key, 6)
    for position, shards_of in cuts:
        draws = jnp.exp(jax.random.uniform(jax.random.fold_in(own, position), (shards_of,), jnp.float32, least / len(cuts), largest / len(cuts)))
        gain = gain * jnp.repeat(draws, dims[position] // shards_of).reshape([-1 if axis == position else 1 for axis in range(len(dims))])
    return gain


def normal_values(rng, extent, deviation, reach, shards=(), kind=jnp.bfloat16):
    entries = jax.random.normal(rng, extent, jnp.float32) * deviation
    if len(shards) > 0:
        entries = level_of(rng, extent, shards, -0.22, 0.18) * entries
    return jnp.clip(entries, min=-reach, max=reach).astype(kind)


def heavy_noise(stream_key, shape, width, reach, cuts, heavy, kind=jnp.bfloat16):
    array = width * jax.random.normal(stream_key, shape, jnp.float32)
    if cuts:
        array = array * level_of(stream_key, shape, cuts, -0.22, 0.18)
    return jnp.clip(raised(array, jax.random.fold_in(stream_key, 3), *heavy), -reach, reach).astype(kind)


def setup_inputs(seed: int = 0) -> dict:
    key_list = jax.random.split(jax.random.key(seed), 12)
    mamba_x = normal_values(key_list[0], (SPAN_OF_INPUT, INNER), 1.0, 6.0, ((0, 16), (1, 2)))
    gate_z = normal_values(key_list[1], (SPAN_OF_INPUT, INNER), 1.0, 6.0, ((0, 16), (1, 2)))
    b_in = normal_values(key_list[2], (SPAN_OF_INPUT, NGROUPS * STATE), (STATE ** -0.5), 1.25, ((0, 16), (1, 2)))
    c_in = normal_values(key_list[3], (SPAN_OF_INPUT, NGROUPS * STATE), (STATE ** -0.5), 1.25, ((0, 16), (1, 2)))
    dt_raw = draw_dt_raw(jax.random.fold_in(key_list[11], 71), 0)
    a_log = draw_a_log(jax.random.fold_in(key_list[11], 71), 0)
    skip_d = jnp.clip(0.5 + 1.0 * jax.random.uniform(key_list[6], (MHEADS,), jnp.float32) ** level_of(key_list[6], (MHEADS,), ((0, 2),), -0.2, 0.2), 0.5, 1.5)
    norm_gain = jnp.clip(1.0 + 0.1 * jax.random.normal(key_list[7], (INNER,), jnp.float32), 0.5, 1.5)
    value_weight = heavy_noise(key_list[8], (INNER, KVHEADS * HEAD_DIM), INNER ** -0.5, 0.09375, ((0, 2),), (0, 1, 2, 2.0))
    queries = draw_queries(jax.random.fold_in(key_list[11], 71), 0)
    keys = draw_keys(jax.random.fold_in(key_list[11], 71), 0)
    return {"mamba_x": mamba_x, "gate_z": gate_z, "b_in": b_in, "c_in": c_in, "dt_raw": dt_raw, "a_log": a_log, "skip_d": skip_d, "norm_gain": norm_gain, "value_weight": value_weight, "queries": queries, "keys": keys}


highest = lax.Precision.HIGHEST
norm_eps = 1e-05

def block_scan(inputs, b_group, c_group, time_step, decay_rate):
    token_count = inputs.shape[0]
    log_decay = jnp.cumsum(-time_step * decay_rate[..., None], axis=2)
    log_gaps = log_decay[..., :, None] - log_decay[..., None, :]
    causal = jnp.arange(token_count)[:, None] >= jnp.arange(token_count)[None, :]
    decay_mat = jnp.exp(jnp.where(causal, log_gaps, -jnp.inf))
    cross_terms = jnp.einsum('tgn,sgn->gts', c_group, b_group, precision=highest)
    mixing = cross_terms[:, None] * decay_mat * time_step[:, :, None, :]
    local_out = jnp.einsum('gkts,sgkp->tgkp', mixing, inputs, precision=highest)
    tail_weight = jnp.exp(log_decay[..., -1:] - log_decay) * time_step
    summary = jnp.einsum('gks,sgkp,sgn->gkpn', tail_weight, inputs, b_group, precision=highest)
    return (log_decay, local_out, summary, jnp.exp(log_decay[..., -1]))

def carried_out(c_group, state_in, log_decay):
    carried_term = jnp.einsum('tgn,gkpn->tgkp', c_group, state_in, precision=highest)
    return carried_term * jnp.transpose(jnp.exp(log_decay), (2, 0, 1))[..., None]

def gated_norm(ssm_out, gate_z, norm_gain, group_count):
    token_count = ssm_out.shape[0]
    gated = ssm_out * jax.nn.silu(gate_z.astype(jnp.float32))
    grouped = gated.reshape(token_count, group_count, -1)
    inverse = lax.rsqrt(lax.optimization_barrier(jnp.mean(grouped * grouped, axis=2, keepdims=True)) + norm_eps)
    return ((grouped * inverse).reshape(token_count, -1) * norm_gain).astype(jnp.bfloat16)

def causal_attention(queries, keys, values):
    per_kv = QHEADS // KVHEADS
    query_block = TOK_DEV * min(N_SEQ, 4)
    block_count = SPAN_OF_INPUT // query_block
    score_scale = 1.0 / math.sqrt(HEAD_DIM)
    query_heads = jnp.transpose(queries.astype(jnp.float32).reshape(SPAN_OF_INPUT, KVHEADS, per_kv, HEAD_DIM), (1, 0, 2, 3))
    key_heads = jnp.transpose(keys.astype(jnp.float32).reshape(SPAN_OF_INPUT, KVHEADS, HEAD_DIM), (1, 0, 2))
    value_heads = jnp.transpose(values.astype(jnp.float32).reshape(SPAN_OF_INPUT, KVHEADS, HEAD_DIM), (1, 0, 2))

    def one_head(head_inputs):
        query_all, key_all, value_all = head_inputs

        def one_block(block_index):
            first_row = (block_index * query_block).astype(jnp.int32)
            query_slab = lax.dynamic_slice_in_dim(query_all, first_row, query_block, 0)
            query_pos = first_row + jnp.arange(query_block, dtype=jnp.int32)

            def block_scores(key_index):
                key_first = (key_index * query_block).astype(jnp.int32)
                key_slab = lax.dynamic_slice_in_dim(key_all, key_first, query_block, 0)
                scores = jnp.einsum('rgd,cd->grc', query_slab, key_slab) * score_scale
                key_pos = key_first + jnp.arange(query_block, dtype=jnp.int32)
                allowed = key_pos[None, :] <= query_pos[:, None]
                return jnp.where(allowed[None], scores, -jnp.inf)

            def find_max(key_index, running_max):
                return jnp.maximum(running_max, lax.optimization_barrier(jnp.max(block_scores(key_index), axis=2)))
            row_max = lax.fori_loop(0, block_index + 1, find_max, jnp.full((per_kv, query_block), -jnp.inf, jnp.float32))

            def accumulate(key_index, running):
                weighted_sum, weight_sum = running
                weights = jnp.exp(block_scores(key_index) - row_max[..., None])
                rounded = lax.optimization_barrier(weights.astype(jnp.bfloat16)).astype(jnp.float32)
                key_first = (key_index * query_block).astype(jnp.int32)
                value_slab = lax.dynamic_slice_in_dim(value_all, key_first, query_block, 0)
                return (weighted_sum + jnp.einsum('grc,cd->grd', rounded, value_slab), weight_sum + lax.optimization_barrier(jnp.sum(weights, axis=2)))
            weighted_sum, weight_sum = lax.fori_loop(0, block_index + 1, accumulate, (jnp.zeros((per_kv, query_block, HEAD_DIM), jnp.float32), jnp.zeros((per_kv, query_block), jnp.float32)))
            return (weighted_sum / weight_sum[..., None]).astype(jnp.bfloat16)
        return lax.map(one_block, jnp.arange(block_count, dtype=jnp.int32))
    outputs = lax.map(one_head, (query_heads, key_heads, value_heads))
    return jnp.transpose(outputs, (1, 3, 0, 2, 4)).reshape(SPAN_OF_INPUT, QHEADS * HEAD_DIM)

def reference(mamba_x, gate_z, b_in, c_in, dt_raw, a_log, skip_d, norm_gain, value_weight, queries, keys):
    per_group = MHEADS // NGROUPS
    inputs_all = mamba_x.astype(jnp.float32).reshape(N_SEQ, TOK_DEV, NGROUPS, per_group, MHEAD_DIM)
    b_all = b_in.astype(jnp.float32).reshape(N_SEQ, TOK_DEV, NGROUPS, STATE)
    c_all = c_in.astype(jnp.float32).reshape(N_SEQ, TOK_DEV, NGROUPS, STATE)
    steps_all = jnp.transpose(jax.nn.softplus(dt_raw).reshape(NGROUPS, per_group, N_SEQ, TOK_DEV), (2, 0, 1, 3))
    decay_rate = jnp.exp(a_log).reshape(NGROUPS, per_group)
    skip_heads = skip_d.reshape(NGROUPS, per_group)[None, :, :, None]

    def advance(carried, block_inputs):
        inputs, b_group, c_group, time_step = block_inputs
        log_decay, local_out, summary, totals = block_scan(inputs, b_group, c_group, time_step, decay_rate)
        ssm_block = local_out + carried_out(c_group, carried, log_decay) + skip_heads * inputs
        return (totals[..., None, None] * carried + summary, ssm_block)
    start_state = jnp.zeros((NGROUPS, per_group, MHEAD_DIM, STATE), jnp.float32)
    _, ssm_blocks = lax.scan(advance, start_state, (inputs_all, b_all, c_all, steps_all))
    ssm_out = ssm_blocks.reshape(SPAN_OF_INPUT, INNER)
    mamba_out = gated_norm(ssm_out, gate_z, norm_gain, NGROUPS)
    values = jnp.dot(mamba_out, value_weight, preferred_element_type=jnp.float32).astype(jnp.bfloat16)
    attention = causal_attention(queries, keys, values)
    return (mamba_out, attention)
```

```python
import functools
import math

import jax
import jax.numpy as jnp
from jax import lax
from jax.experimental import pallas as pl
from jax.experimental.pallas import tpu as pltpu
from jax.sharding import PartitionSpec as P

MHEAD_DIM = 64
STATE = 128
GROUP_HEADS = 16
QHEADS = 32
KVHEADS = 8
HEAD_DIM = 128
PLANE = 4
BLOCK = 128
NORM_EPS = 1e-05

MESH = pl.DeviceIdType.MESH
HIGHEST = lax.Precision.HIGHEST
f32 = jnp.float32
bf16 = jnp.bfloat16


def dot(a, b, ca=1, cb=0, precision=None):
    return lax.dot_general(
        a, b, (((ca,), (cb,)), ((), ())), precision=precision, preferred_element_type=f32
    )


def kernel(
    n_seq, n_tp,
    x_ref, z_ref, b_ref, c_ref, dt_ref, alog_ref, skip_ref, gain_ref, w_hbm, q_ref, k_ref,
    mo_ref, att_ref,
    w_ref, xo, bo, co, dto, qo, ko, vo, sin, sout, yo, yh, part, vp, scores, probs, sums, ao, loc, scale_out,
    w_sem, own_sem, a_send, a_recv, k_send, k_recv, c_send, c_recv, y_send, y_recv,
    p_send, p_recv, v_send, v_recv, o_send, o_recv,
):
    tok, chans = x_ref.shape
    lanes = chans // PLANE
    heads = lanes // MHEAD_DIM
    nz = n_seq // PLANE
    span = PLANE * tok
    kv_here = k_ref.shape[1] // HEAD_DIM
    q_lanes = q_ref.shape[1] // PLANE
    q_heads = q_lanes // HEAD_DIM
    groups = b_ref.shape[1] // STATE
    seq = lax.axis_index("seq")
    t = lax.axis_index("tp")
    z = seq // PLANE
    p = seq % PLANE

    def seq_id(zz, pp):
        return zz * PLANE + pp

    def cols(index, width):
        return pl.ds(pl.multiple_of(index * width, width), width)

    load_w = pltpu.make_async_copy(w_hbm, w_ref, w_sem)
    load_w.start()

    barrier = pltpu.get_barrier_semaphore()
    for dt_ in range(n_tp):
        for dp in range(PLANE):
            if dt_ or dp:
                pl.semaphore_signal(
                    barrier, inc=1,
                    device_id=(seq_id(z, (p + dp) % PLANE), (t + dt_) % n_tp), device_id_type=MESH,
                )
    for dz in range(1, nz):
        pl.semaphore_signal(
            barrier, inc=1, device_id=(seq_id((z + dz) % nz, p), t), device_id_type=MESH
        )
    pl.semaphore_wait(barrier, n_tp * PLANE - 1 + nz - 1)

    def pieces(to, slot):
        group = to * groups // PLANE
        kv = to * kv_here // PLANE
        return (
            (x_ref.at[:, cols(to, lanes)], xo.at[slot]),
            (b_ref.at[:, cols(group, STATE)], bo.at[slot]),
            (dt_ref.at[to], dto.at[slot]),
            (c_ref.at[:, cols(group, STATE)], co.at[slot]),
            (k_ref.at[:, cols(kv, HEAD_DIM)], ko.at[z, slot]),
            (q_ref.at[:, cols(to, q_lanes)], qo.at[slot]),
        )

    def exchange(d, i, src, dst):
        return pltpu.make_async_remote_copy(
            src_ref=src, dst_ref=dst, send_sem=a_send.at[i, d], recv_sem=a_recv.at[i, d],
            device_id=(seq_id(z, (p + d) % PLANE), t), device_id_type=MESH,
        )

    sends = {}
    for i in range(6):
        for d in range(1, PLANE):
            src, dst = pieces((p + d) % PLANE, p)[i]
            sends[i, d] = exchange(d, i, src, dst)
            sends[i, d].start()
        src, dst = pieces(p, p)[i]
        sends[i, 0] = pltpu.make_async_copy(src, dst, own_sem.at[i])
        sends[i, 0].start()

    def arrived(i):
        for d in range(1, PLANE):
            src, dst = pieces(p, (p + PLANE - d) % PLANE)[i]
            exchange(d, i, src, dst).wait_recv()
        sends[i, 0].wait()

    for i in range(4):
        arrived(i)

    rate = jnp.exp(alog_ref[p])
    spread = (
        lax.broadcasted_iota(jnp.int32, (heads, lanes), 1) // MHEAD_DIM
        == lax.broadcasted_iota(jnp.int32, (heads, lanes), 0)
    ).astype(f32)
    row = lax.broadcasted_iota(jnp.int32, (tok, BLOCK), 0)
    col = lax.broadcasted_iota(jnp.int32, (tok, BLOCK), 1)
    causal = (
        lax.broadcasted_iota(jnp.int32, (BLOCK, BLOCK), 0)
        >= lax.broadcasted_iota(jnp.int32, (BLOCK, BLOCK), 1)
    )
    left_half = lax.broadcasted_iota(jnp.int32, (BLOCK, BLOCK), 1) < MHEAD_DIM
    per_block = BLOCK // tok
    n_blocks = span // BLOCK
    decay_in, added = [], []
    factors = []
    for blk in range(n_blocks):
        l_row = l_col = t_row = t_col = 0.0
        for j in range(per_block):
            raw = dto[blk * per_block + j]
            step = jnp.maximum(raw, 0.0) + jnp.log1p(jnp.exp(-jnp.abs(raw)))
            log_step = -step * rate
            upto = (row + j * tok <= col).astype(f32)
            same = (row + j * tok == col).astype(f32)
            l_row += dot(log_step, upto, precision=HIGHEST)
            l_col += dot(upto, log_step, 0, 1, precision=HIGHEST)
            t_row += dot(step, same, precision=HIGHEST)
            t_col += dot(same, step, 0, 1, precision=HIGHEST)
        tail = jnp.exp(l_col[BLOCK - 1 :, :] - l_col) * t_col
        grown = dot(jnp.exp(l_col), spread, precision=HIGHEST)
        scale_out[blk] = grown
        xb = xo[pl.ds(blk * per_block, per_block)].reshape(BLOCK, lanes)
        bb = bo[pl.ds(blk * per_block, per_block)].reshape(BLOCK, STATE)
        weighted = (xb.astype(f32) * dot(tail, spread, precision=HIGHEST)).astype(bf16)
        added.append(dot(bb, weighted, 0, 0))
        decay_in.append(grown[BLOCK - 1 :, :])
        factors.append((l_row, l_col, t_row, xb, bb))
    before = [(jnp.ones((1, lanes), f32), jnp.zeros((STATE, lanes), f32))]
    for blk in range(n_blocks):
        dec, own = before[-1]
        before.append((dec * decay_in[blk], decay_in[blk] * own + added[blk]))
    plane_dec, plane_own = before[-1]

    n_chunks, _, width = sin.shape

    def chain(i, src, dst):
        return pltpu.make_async_remote_copy(
            src_ref=src, dst_ref=dst, send_sem=c_send.at[i], recv_sem=c_recv.at[i],
            device_id=(seq_id((z + 1) % nz, p), t), device_id_type=MESH,
        )

    @pl.when(z == 0)
    def _():
        sin[...] = jnp.zeros_like(sin)
        for i in range(n_chunks):
            sout[i] = plane_own[:, i * width : (i + 1) * width]
            chain(i, sout.at[i], sin.at[i]).start()

    for blk in range(n_blocks):
        l_row, l_col, t_row, xb, bb = factors[blk]
        cb = co[pl.ds(blk * per_block, per_block)].reshape(BLOCK, STATE)
        cross = dot(cb, bb, 1, 1)
        for pair in range(heads // 2):
            mixes = []
            for h in (2 * pair, 2 * pair + 1):
                gaps = jnp.where(causal, l_col[:, h : h + 1] - l_row[h : h + 1, :], -jnp.inf)
                mixes.append((cross * jnp.exp(gaps) * t_row[h : h + 1, :]).astype(bf16))
            both = dot(jnp.concatenate(mixes, axis=0), xb[:, pair * BLOCK : (pair + 1) * BLOCK])
            loc[blk, :, pair * BLOCK : (pair + 1) * BLOCK] = jnp.where(
                left_half, both[:BLOCK], both[BLOCK:]
            )

    @pl.when(z > 0)
    def _():
        for i in range(n_chunks):
            chain(i, sout.at[i], sin.at[i]).wait_recv()

            @pl.when(z < nz - 1)
            def _():
                part_cols = slice(i * width, (i + 1) * width)
                sout[i] = plane_dec[:, part_cols] * sin[i] + plane_own[:, part_cols]
                chain(i, sout.at[i], sin.at[i]).start()

    skip = dot(jnp.broadcast_to(skip_ref[p], (8, heads)), spread, precision=HIGHEST)[:1]
    for blk in range(n_blocks):
        cb = co[pl.ds(blk * per_block, per_block)].reshape(BLOCK, STATE)
        dec, own = before[blk]
        for i in range(n_chunks):
            pc = slice(i * width, (i + 1) * width)
            state = dec[:, pc] * sin[i] + own[:, pc]
            high = state.astype(bf16)
            low = (state - high.astype(f32)).astype(bf16)
            y = (
                loc[blk, :, pc]
                + scale_out[blk, :, pc] * (dot(cb, high) + dot(cb, low))
                + skip[:, pc] * factors[blk][3][:, pc].astype(f32)
            )
            yo[pl.ds(blk * per_block, per_block), :, pc] = y.astype(bf16).reshape(
                per_block, tok, width
            )

    def give_back(d):
        return pltpu.make_async_remote_copy(
            src_ref=yo.at[(p + d) % PLANE], dst_ref=yh.at[p],
            send_sem=y_send.at[d], recv_sem=y_recv.at[d],
            device_id=(seq_id(z, (p + d) % PLANE), t), device_id_type=MESH,
        )

    for d in range(1, PLANE):
        give_back(d).start()
    yh[p] = yo[p]

    arrived(4)
    arrived(5)

    def later(buffer, zz, send, recv):
        return pltpu.make_async_remote_copy(
            src_ref=buffer.at[z], dst_ref=buffer.at[z], send_sem=send.at[zz], recv_sem=recv.at[z],
            device_id=(seq_id(zz, p), t), device_id_type=MESH,
        )

    def earlier(buffer, zz, send, recv):
        return pltpu.make_async_remote_copy(
            src_ref=buffer.at[zz], dst_ref=buffer.at[zz], send_sem=send.at[zz], recv_sem=recv.at[zz],
            device_id=(seq_id(zz, p), t), device_id_type=MESH,
        )

    def push(buffer, send, recv):
        for zz in range(1, nz):
            @pl.when(zz > z)
            def _():
                later(buffer, zz, send, recv).start()

    def pushed(buffer, send, recv):
        for zz in range(1, nz):
            @pl.when(zz > z)
            def _():
                later(buffer, zz, send, recv).wait_send()

    def take(buffer, send, recv):
        for zz in range(nz - 1):
            @pl.when(zz < z)
            def _():
                earlier(buffer, zz, send, recv).wait_recv()

    push(ko, k_send, k_recv)
    take(ko, k_send, k_recv)
    within = (
        lax.broadcasted_iota(jnp.int32, (span, span), 0)
        >= lax.broadcasted_iota(jnp.int32, (span, span), 1)
    )
    score_scale = 1.0 / math.sqrt(HEAD_DIM)
    for h in range(q_heads):
        query = qo[:, :, h * HEAD_DIM : (h + 1) * HEAD_DIM].reshape(span, HEAD_DIM)
        own_scores = jnp.where(
            within, dot(query, ko[z].reshape(span, HEAD_DIM), 1, 1) * score_scale, -jnp.inf
        )

        def score(zz, largest):
            s = dot(query, ko[zz].reshape(span, HEAD_DIM), 1, 1) * score_scale
            scores[zz] = s
            return jnp.maximum(largest, jnp.max(s, axis=1, keepdims=True))

        largest = lax.fori_loop(0, z, score, jnp.max(own_scores, axis=1, keepdims=True))
        weights = jnp.exp(own_scores - largest)
        probs[z, h] = weights.astype(bf16)

        def weigh(zz, total):
            e = jnp.exp(scores[zz] - largest)
            probs[zz, h] = e.astype(bf16)
            return total + jnp.sum(e, axis=1, keepdims=True)

        total = lax.fori_loop(0, z, weigh, jnp.sum(weights, axis=1, keepdims=True))
        sums[h] = jnp.broadcast_to(total, (span, HEAD_DIM))

    for d in range(1, PLANE):
        give_back(d).wait_recv()
    group_lanes = chans // groups
    for g in range(groups):
        gc = slice(g * group_lanes, (g + 1) * group_lanes)
        if group_lanes == lanes:
            ssm = yh[g].astype(f32)
        else:
            ssm = jnp.concatenate([yh[j].astype(f32) for j in range(PLANE)], axis=1)
        zg = z_ref[:, gc].astype(f32)
        gated = ssm * (zg / (1.0 + jnp.exp(-zg)))
        inverse = lax.rsqrt(jnp.mean(gated * gated, axis=1, keepdims=True) + NORM_EPS)
        mo_ref[:, gc] = (gated * inverse * gain_ref[:, gc]).astype(bf16)
    load_w.wait()
    for n in range(w_ref.shape[1] // 256):
        product = dot(mo_ref[...], w_ref[:, n * 256 : (n + 1) * 256]).astype(bf16)
        part[2 * n] = product[:, :HEAD_DIM]
        part[2 * n + 1] = product[:, HEAD_DIM:]

    def partial_copy(dt_, dp):
        tt, pp = (t + dt_) % n_tp, (p + dp) % PLANE
        return pltpu.make_async_remote_copy(
            src_ref=part.at[tt * kv_here + pp * kv_here // PLANE], dst_ref=vp.at[t, p],
            send_sem=p_send.at[dt_, dp], recv_sem=p_recv.at[dt_, dp],
            device_id=(seq_id(z, pp), tt), device_id_type=MESH,
        )

    offsets = [(dt_, dp) for dt_ in range(n_tp) for dp in range(PLANE) if dt_ or dp]
    for dt_, dp in offsets:
        partial_copy(dt_, dp).start()
    vp[t, p] = part[t * kv_here + p * kv_here // PLANE]
    for dt_, dp in offsets:
        partial_copy(dt_, dp).wait_recv()
    values = vp[0].astype(f32)
    for tt in range(1, n_tp):
        values = values + vp[tt].astype(f32)
    vo[z] = values.astype(bf16)
    push(vo, v_send, v_recv)
    outs = [
        dot(probs[z, h], vo[z].reshape(span, HEAD_DIM)) for h in range(q_heads)
    ]
    take(vo, v_send, v_recv)
    for h in range(q_heads):
        def gather(zz, acc):
            return acc + dot(probs[zz, h], vo[zz].reshape(span, HEAD_DIM))

        acc = lax.fori_loop(0, z, gather, outs[h])
        ao[:, :, h * HEAD_DIM : (h + 1) * HEAD_DIM] = (
            (acc / sums[h]).astype(bf16).reshape(PLANE, tok, HEAD_DIM)
        )

    def hand_out(d):
        return pltpu.make_async_remote_copy(
            src_ref=ao.at[(p + d) % PLANE], dst_ref=att_ref.at[:, cols(p, q_lanes)],
            send_sem=o_send.at[d], recv_sem=o_recv.at[d],
            device_id=(seq_id(z, (p + d) % PLANE), t), device_id_type=MESH,
        )

    for d in range(1, PLANE):
        hand_out(d).start()
    att_ref[:, cols(p, q_lanes)] = ao[p]

    for i in range(6):
        for d in range(1, PLANE):
            sends[i, d].wait_send()
    @pl.when(z < nz - 1)
    def _():
        for i in range(n_chunks):
            chain(i, sout.at[i], sin.at[i]).wait_send()
    for d in range(1, PLANE):
        give_back(d).wait_send()
    pushed(ko, k_send, k_recv)
    pushed(vo, v_send, v_recv)
    for dt_, dp in offsets:
        partial_copy(dt_, dp).wait_send()
    for d in range(1, PLANE):
        hand_out(d).wait_recv()
        hand_out(d).wait_send()


def per_device(
    n_seq, n_tp,
    mamba_x, gate_z, b_in, c_in, dt_raw, a_log, skip_d, norm_gain, value_weight, queries, keys,
):
    tok, chans = mamba_x.shape
    lanes = chans // PLANE
    heads = lanes // MHEAD_DIM
    nz = n_seq // PLANE
    span = PLANE * tok
    q_lanes = queries.shape[1] // PLANE
    q_heads = q_lanes // HEAD_DIM
    width = min(128, lanes)
    n_chunks = lanes // width
    vmem = pl.BlockSpec(memory_space=pltpu.VMEM)
    dma = pltpu.SemaphoreType.DMA
    return pl.pallas_call(
        functools.partial(kernel, n_seq, n_tp),
        out_shape=(
            jax.ShapeDtypeStruct((tok, chans), bf16),
            jax.ShapeDtypeStruct(queries.shape, bf16),
        ),
        in_specs=[vmem] * 8 + [pl.BlockSpec(memory_space=pl.ANY)] + [vmem] * 2,
        out_specs=(vmem, vmem),
        scratch_shapes=[
            pltpu.VMEM(value_weight.shape, bf16),
            pltpu.VMEM((PLANE, tok, lanes), bf16),
            pltpu.VMEM((PLANE, tok, STATE), bf16),
            pltpu.VMEM((PLANE, tok, STATE), bf16),
            pltpu.VMEM((PLANE, heads, tok), f32),
            pltpu.VMEM((PLANE, tok, q_lanes), bf16),
            pltpu.VMEM((nz, PLANE, tok, HEAD_DIM), bf16),
            pltpu.VMEM((nz, PLANE, tok, HEAD_DIM), bf16),
            pltpu.VMEM((n_chunks, STATE, width), f32),
            pltpu.VMEM((n_chunks, STATE, width), f32),
            pltpu.VMEM((PLANE, tok, lanes), bf16),
            pltpu.VMEM((PLANE, tok, lanes), bf16),
            pltpu.VMEM((KVHEADS, tok, HEAD_DIM), bf16),
            pltpu.VMEM((n_tp, PLANE, tok, HEAD_DIM), bf16),
            pltpu.VMEM((nz, span, span), f32),
            pltpu.VMEM((nz, q_heads, span, span), bf16),
            pltpu.VMEM((q_heads, span, HEAD_DIM), f32),
            pltpu.VMEM((PLANE, tok, q_lanes), bf16),
            pltpu.VMEM((span // BLOCK, BLOCK, lanes), f32),
            pltpu.VMEM((span // BLOCK, BLOCK, lanes), f32),
            dma, dma((6,)),
            dma((6, PLANE)), dma((6, PLANE)),
            dma((nz,)), dma((nz,)),
            dma((n_chunks,)), dma((n_chunks,)),
            dma((PLANE,)), dma((PLANE,)),
            dma((n_tp, PLANE)), dma((n_tp, PLANE)),
            dma((nz,)), dma((nz,)),
            dma((PLANE,)), dma((PLANE,)),
        ],
        compiler_params=pltpu.CompilerParams(
            collective_id=0, has_side_effects=True, vmem_limit_bytes=52 * 1024 * 1024
        ),
    )(
        mamba_x, gate_z, b_in, c_in,
        dt_raw.reshape(PLANE, heads, tok), a_log.reshape(PLANE, heads, 1),
        skip_d.reshape(PLANE, 1, heads), norm_gain.reshape(1, chans), value_weight, queries, keys,
    )


def solution(mesh):
    placed = (
        P("seq", "tp"),
        P("seq", "tp"),
        P("seq", "tp"),
        P("seq", "tp"),
        P("tp", "seq"),
        P("tp"),
        P("tp"),
        P("tp"),
        P("tp", None),
        P("seq", "tp"),
        P("seq", "tp"),
    )
    return jax.shard_map(
        functools.partial(per_device, mesh.shape["seq"], mesh.shape["tp"]),
        mesh=mesh,
        in_specs=placed,
        out_specs=(P("seq", "tp"), P("seq", "tp")),
        check_vma=False,
    )
```

```python
import functools
import math

import jax
import jax.numpy as jnp
from jax import lax
from jax.experimental import pallas as pl
from jax.experimental.pallas import tpu as pltpu
from jax.sharding import PartitionSpec as P

MHEAD_DIM = 64
STATE = 128
GROUP_HEADS = 16
QHEADS = 32
KVHEADS = 8
HEAD_DIM = 128
PLANE = 4
BLOCK = 128
NORM_EPS = 1e-05

MESH = pl.DeviceIdType.MESH
f32 = jnp.float32
bf16 = jnp.bfloat16


def dot(a, b, ca=1, cb=0):
    return lax.dot_general(a, b, (((ca,), (cb,)), ((), ())), preferred_element_type=f32)


def kernel(
    n_seq, n_tp,
    x_hbm, z_hbm, b_hbm, c_hbm, dt_hbm, alog_ref, skip_ref, gain_ref, w_hbm, q_hbm, k_hbm,
    mo_ref, att_ref,
    w_ref, z_ref, xo, bo, co, dto, qo, ko, vo, sin, sout, yo, yh, part, vp, scores, probs, sums, accs, ao,
    grown, tail_w, silu,
    w_sem, z_sem, own_sem, a_send, a_recv, k_send, k_recv, c_send, c_recv, y_send, y_recv,
    p_send, p_recv, v_send, v_recv, o_send, o_recv,
):
    tok, chans = x_hbm.shape
    lanes = chans // PLANE
    heads = lanes // MHEAD_DIM
    nz = n_seq // PLANE
    span = PLANE * tok
    kv_here = k_hbm.shape[1] // HEAD_DIM
    q_lanes = q_hbm.shape[1] // PLANE
    q_heads = q_lanes // HEAD_DIM
    groups = b_hbm.shape[1] // STATE
    seq = lax.axis_index("seq")
    t = lax.axis_index("tp")
    z = seq // PLANE
    p = seq % PLANE

    def seq_id(zz, pp):
        return zz * PLANE + pp

    def cols(index, width):
        return pl.ds(pl.multiple_of(index * width, width), width)

    barrier = pltpu.get_barrier_semaphore()
    for dt_ in range(n_tp):
        for dp in range(PLANE):
            if dt_ or dp:
                pl.semaphore_signal(
                    barrier, inc=1,
                    device_id=(seq_id(z, (p + dp) % PLANE), (t + dt_) % n_tp), device_id_type=MESH,
                )
    for dz in range(1, nz):
        pl.semaphore_signal(
            barrier, inc=1, device_id=(seq_id((z + dz) % nz, p), t), device_id_type=MESH
        )

    def pieces(to, slot):
        group = to * groups // PLANE
        kv = to * kv_here // PLANE
        return (
            (k_hbm.at[:, cols(kv, HEAD_DIM)], ko.at[z, slot]),
            (dt_hbm.at[to], dto.at[slot]),
            (b_hbm.at[:, cols(group, STATE)], bo.at[slot]),
            (x_hbm.at[:, cols(to, lanes)], xo.at[slot]),
            (c_hbm.at[:, cols(group, STATE)], co.at[slot]),
            (q_hbm.at[:, cols(to, q_lanes)], qo.at[slot]),
        )

    def exchange(d, i, src, dst):
        return pltpu.make_async_remote_copy(
            src_ref=src, dst_ref=dst, send_sem=a_send.at[i, d], recv_sem=a_recv.at[i, d],
            device_id=(seq_id(z, (p + d) % PLANE), t), device_id_type=MESH,
        )

    sends = {}
    for i in range(6):
        src, dst = pieces(p, p)[i]
        sends[i, 0] = pltpu.make_async_copy(src, dst, own_sem.at[i])
        sends[i, 0].start()
    pl.semaphore_wait(barrier, n_tp * PLANE - 1 + nz - 1)
    for i in range(6):
        for d in range(1, PLANE):
            src, dst = pieces((p + d) % PLANE, p)[i]
            sends[i, d] = exchange(d, i, src, dst)
            sends[i, d].start()
    load_z = pltpu.make_async_copy(z_hbm, z_ref, z_sem)
    load_z.start()
    load_w = pltpu.make_async_copy(w_hbm, w_ref, w_sem)
    load_w.start()

    def arrived(i):
        for d in range(1, PLANE):
            src, dst = pieces(p, (p + PLANE - d) % PLANE)[i]
            exchange(d, i, src, dst).wait_recv()
        sends[i, 0].wait()

    def later(buffer, zz, send, recv):
        return pltpu.make_async_remote_copy(
            src_ref=buffer.at[z], dst_ref=buffer.at[z], send_sem=send.at[zz], recv_sem=recv.at[z],
            device_id=(seq_id(zz, p), t), device_id_type=MESH,
        )

    def earlier(buffer, zz, send, recv):
        return pltpu.make_async_remote_copy(
            src_ref=buffer.at[zz], dst_ref=buffer.at[zz], send_sem=send.at[zz], recv_sem=recv.at[zz],
            device_id=(seq_id(zz, p), t), device_id_type=MESH,
        )

    def push(buffer, send, recv):
        for zz in range(1, nz):
            @pl.when(zz > z)
            def _():
                later(buffer, zz, send, recv).start()

    def pushed(buffer, send, recv):
        for zz in range(1, nz):
            @pl.when(zz > z)
            def _():
                later(buffer, zz, send, recv).wait_send()

    arrived(0)
    push(ko, k_send, k_recv)

    arrived(1)
    per_block = BLOCK // tok
    n_blocks = span // BLOCK
    rows = n_blocks * heads
    head_row = lax.broadcasted_iota(jnp.int32, (heads, BLOCK), 0)
    log_rate = jnp.zeros((heads, BLOCK), f32)
    for h in range(heads):
        log_rate = jnp.where(head_row == h, alog_ref[0, p * heads + h], log_rate)
    raw = jnp.concatenate(
        [
            jnp.concatenate([dto[blk * per_block + j] for j in range(per_block)], axis=1)
            for blk in range(n_blocks)
        ],
        axis=0,
    )
    steps = jnp.maximum(raw, 0.0) + jnp.log1p(jnp.exp(-jnp.abs(raw)))
    log_step = -steps * jnp.concatenate([jnp.exp(log_rate)] * n_blocks, axis=0)
    row = lax.broadcasted_iota(jnp.int32, (BLOCK, BLOCK), 0)
    col = lax.broadcasted_iota(jnp.int32, (BLOCK, BLOCK), 1)
    causal = row >= col
    left_half = col < MHEAD_DIM
    upto = (row <= col).astype(bf16)
    first = log_step.astype(bf16).astype(f32)
    second = (log_step - first).astype(bf16).astype(f32)
    third = log_step - first - second
    summed = dot(jnp.concatenate([first, second, third], axis=0).astype(bf16), upto)
    l_rows = summed[:rows] + summed[rows : 2 * rows] + summed[2 * rows :]
    turned = jnp.concatenate([l_rows, steps, jnp.zeros((BLOCK - 2 * rows, BLOCK), f32)], axis=0).T

    def column(kind, blk, h):
        at = kind * rows + blk * heads + h
        return jnp.broadcast_to(turned[:, at : at + 1], (BLOCK, BLOCK))

    n_chunks = sin.shape[0]
    for blk in range(n_blocks):
        for i in range(n_chunks):
            l_both = jnp.where(left_half, column(0, blk, 2 * i), column(0, blk, 2 * i + 1))
            t_both = jnp.where(left_half, column(1, blk, 2 * i), column(1, blk, 2 * i + 1))
            grown[blk, i] = jnp.exp(l_both)
            tail_w[blk, i] = jnp.exp(l_both[BLOCK - 1 :, :] - l_both) * t_both

    def chain(i):
        return pltpu.make_async_remote_copy(
            src_ref=sout.at[i], dst_ref=sin.at[i], send_sem=c_send.at[i], recv_sem=c_recv.at[i],
            device_id=(seq_id((z + 1) % nz, p), t), device_id_type=MESH,
        )

    def chunk(i):
        return slice(i * BLOCK, (i + 1) * BLOCK)

    arrived(2)
    arrived(3)
    b_blocks = [
        bo[pl.ds(blk * per_block, per_block)].reshape(BLOCK, STATE) for blk in range(n_blocks)
    ]

    def x_block(blk, i):
        return xo[pl.ds(blk * per_block, per_block), :, chunk(i)].reshape(BLOCK, BLOCK)

    before = {}
    for i in range(n_chunks):
        dec, own = jnp.ones((1, BLOCK), f32), jnp.zeros((STATE, BLOCK), f32)
        for blk in range(n_blocks):
            before[blk, i] = (dec, own)
            weighted = (x_block(blk, i).astype(f32) * tail_w[blk, i]).astype(bf16)
            fade = grown[blk, i, BLOCK - 1 :, :]
            own = fade * own + dot(b_blocks[blk], weighted, 0, 0)
            dec = dec * fade
        before[n_blocks, i] = (dec, own)
        sout[i] = own

        @pl.when(z == 0)
        def _():
            chain(i).start()

    @pl.when(z == 0)
    def _():
        sin[...] = jnp.zeros_like(sin)

    arrived(4)
    c_blocks = [
        co[pl.ds(blk * per_block, per_block)].reshape(BLOCK, STATE) for blk in range(n_blocks)
    ]
    cross = [dot(c_blocks[blk], b_blocks[blk], 1, 1) for blk in range(n_blocks)]

    def give_back(i, d):
        return pltpu.make_async_remote_copy(
            src_ref=yo.at[i, (p + d) % PLANE], dst_ref=yh.at[i, p],
            send_sem=y_send.at[i, d], recv_sem=y_recv.at[i, d],
            device_id=(seq_id(z, (p + d) % PLANE), t), device_id_type=MESH,
        )

    within = (
        lax.broadcasted_iota(jnp.int32, (span, span), 0)
        >= lax.broadcasted_iota(jnp.int32, (span, span), 1)
    )
    score_scale = 1.0 / math.sqrt(HEAD_DIM)

    def attend(h):
        query = qo[:, :, h * HEAD_DIM : (h + 1) * HEAD_DIM].reshape(span, HEAD_DIM)
        own_scores = jnp.where(
            within, dot(query, ko[z].reshape(span, HEAD_DIM), 1, 1) * score_scale, -jnp.inf
        )

        def score(zz, largest):
            s = dot(query, ko[zz].reshape(span, HEAD_DIM), 1, 1) * score_scale
            scores[zz] = s
            return jnp.maximum(largest, jnp.max(s, axis=1, keepdims=True))

        largest = lax.fori_loop(0, z, score, jnp.max(own_scores, axis=1, keepdims=True))
        weights = jnp.exp(own_scores - largest)
        probs[z, h] = weights.astype(bf16)

        def weigh(zz, total):
            e = jnp.exp(scores[zz] - largest)
            probs[zz, h] = e.astype(bf16)
            return total + jnp.sum(e, axis=1, keepdims=True)

        total = lax.fori_loop(0, z, weigh, jnp.sum(weights, axis=1, keepdims=True))
        sums[h] = jnp.broadcast_to(total, (span, HEAD_DIM))

    attended = 0
    for i in range(n_chunks):
        @pl.when(z > 0)
        def _():
            chain(i).wait_recv()

            @pl.when(z < nz - 1)
            def _():
                dec, own = before[n_blocks, i]
                sout[i] = dec * sin[i] + sout[i]
                chain(i).start()

        skip = jnp.where(
            left_half, skip_ref[0, p * heads + 2 * i], skip_ref[0, p * heads + 2 * i + 1]
        )
        for blk in range(n_blocks):
            mixes = []
            for h in (2 * i, 2 * i + 1):
                at = blk * heads + h
                gaps = jnp.where(causal, column(0, blk, h) - l_rows[at : at + 1, :], -jnp.inf)
                mixes.append((cross[blk] * jnp.exp(gaps) * steps[at : at + 1, :]).astype(bf16))
            xb = x_block(blk, i)
            both = dot(jnp.concatenate(mixes, axis=0), xb)
            local = jnp.where(left_half, both[:BLOCK], both[BLOCK:])
            dec, own = before[blk, i]
            state = dec * sin[i] + own
            high = state.astype(bf16)
            low = (state - high.astype(f32)).astype(bf16)
            carried = dot(c_blocks[blk], high) + dot(c_blocks[blk], low)
            y = local + grown[blk, i] * carried + skip * xb.astype(f32)
            yo[i, pl.ds(blk * per_block, per_block)] = y.astype(bf16).reshape(
                per_block, tok, BLOCK
            )
        for d in range(1, PLANE):
            give_back(i, d).start()
        yh[i, p] = yo[i, p]
        while attended < q_heads and (attended + 1) * n_chunks <= (i + 1) * q_heads:
            if attended == 0:
                arrived(5)
                for zz in range(nz - 1):
                    @pl.when(zz < z)
                    def _():
                        earlier(ko, zz, k_send, k_recv).wait_recv()
            attend(attended)
            attended += 1

    load_z.wait()
    zg = z_ref[...].astype(f32)
    silu[...] = zg / (1.0 + jnp.exp(-zg))
    for i in range(n_chunks):
        for d in range(1, PLANE):
            give_back(i, d).wait_recv()
    group_lanes = chans // groups
    for g in range(groups):
        gc = slice(g * group_lanes, (g + 1) * group_lanes)
        owners = range(g * PLANE // groups, (g + 1) * PLANE // groups)
        ssm = jnp.concatenate([yh[i, j] for j in owners for i in range(n_chunks)], axis=1)
        gated = ssm.astype(f32) * silu[:, gc]
        inverse = lax.rsqrt(jnp.mean(gated * gated, axis=1, keepdims=True) + NORM_EPS)
        mo_ref[:, gc] = (gated * inverse * gain_ref[:, gc]).astype(bf16)

    def partial_copy(dt_, dp):
        tt, pp = (t + dt_) % n_tp, (p + dp) % PLANE
        return pltpu.make_async_remote_copy(
            src_ref=part.at[tt * kv_here + pp * kv_here // PLANE], dst_ref=vp.at[t, p],
            send_sem=p_send.at[dt_, dp], recv_sem=p_recv.at[dt_, dp],
            device_id=(seq_id(z, pp), tt), device_id_type=MESH,
        )

    offsets = [(dt_, dp) for dt_ in range(n_tp) for dp in range(PLANE) if dt_ or dp]
    load_w.wait()
    for n in range(w_ref.shape[1] // 256):
        product = dot(mo_ref[...], w_ref[:, n * 256 : (n + 1) * 256]).astype(bf16)
        part[2 * n] = product[:, :HEAD_DIM]
        part[2 * n + 1] = product[:, HEAD_DIM:]
        for dt_, dp in offsets:
            tt, pp = (t + dt_) % n_tp, (p + dp) % PLANE

            @pl.when((tt * kv_here + pp * kv_here // PLANE) // 2 == n)
            def _():
                partial_copy(dt_, dp).start()

    vp[t, p] = part[t * kv_here + p * kv_here // PLANE]
    accs[...] = jnp.zeros_like(accs)

    def take(zz):
        earlier(vo, zz, v_send, v_recv).wait_recv()
        for h in range(q_heads):
            accs[h] += dot(probs[zz, h], vo[zz].reshape(span, HEAD_DIM))

    for zz in range(nz - 2):
        @pl.when(zz < z - 1)
        def _():
            take(zz)

    for dt_, dp in offsets:
        partial_copy(dt_, dp).wait_recv()
    values = vp[0].astype(f32)
    for tt in range(1, n_tp):
        values = values + vp[tt].astype(f32)
    vo[z] = values.astype(bf16)
    push(vo, v_send, v_recv)

    for zz in range(nz - 1):
        @pl.when(zz == z - 1)
        def _():
            take(zz)

    def hand_out(h, d):
        return pltpu.make_async_remote_copy(
            src_ref=ao.at[h, (p + d) % PLANE], dst_ref=att_ref.at[:, cols(p * q_heads + h, HEAD_DIM)],
            send_sem=o_send.at[h, d], recv_sem=o_recv.at[h, d],
            device_id=(seq_id(z, (p + d) % PLANE), t), device_id_type=MESH,
        )

    for h in range(q_heads):
        acc = accs[h] + dot(probs[z, h], vo[z].reshape(span, HEAD_DIM))
        ao[h] = (acc / sums[h]).astype(bf16).reshape(PLANE, tok, HEAD_DIM)
        for d in range(1, PLANE):
            hand_out(h, d).start()
        att_ref[:, cols(p * q_heads + h, HEAD_DIM)] = ao[h, p]

    for i in range(6):
        for d in range(1, PLANE):
            sends[i, d].wait_send()

    @pl.when(z < nz - 1)
    def _():
        for i in range(n_chunks):
            chain(i).wait_send()

    for i in range(n_chunks):
        for d in range(1, PLANE):
            give_back(i, d).wait_send()
    pushed(ko, k_send, k_recv)
    pushed(vo, v_send, v_recv)
    for dt_, dp in offsets:
        partial_copy(dt_, dp).wait_send()
    for h in range(q_heads):
        for d in range(1, PLANE):
            hand_out(h, d).wait_recv()
            hand_out(h, d).wait_send()


def per_device(
    n_seq, n_tp,
    mamba_x, gate_z, b_in, c_in, dt_raw, a_log, skip_d, norm_gain, value_weight, queries, keys,
):
    tok, chans = mamba_x.shape
    lanes = chans // PLANE
    heads = lanes // MHEAD_DIM
    nz = n_seq // PLANE
    span = PLANE * tok
    q_lanes = queries.shape[1] // PLANE
    q_heads = q_lanes // HEAD_DIM
    n_chunks = lanes // BLOCK
    n_blocks = span // BLOCK
    vmem = pl.BlockSpec(memory_space=pltpu.VMEM)
    smem = pl.BlockSpec(memory_space=pltpu.SMEM)
    hbm = pl.BlockSpec(memory_space=pl.ANY)
    dma = pltpu.SemaphoreType.DMA
    return pl.pallas_call(
        functools.partial(kernel, n_seq, n_tp),
        out_shape=(
            jax.ShapeDtypeStruct((tok, chans), bf16),
            jax.ShapeDtypeStruct(queries.shape, bf16),
        ),
        in_specs=[hbm] * 5 + [smem] * 2 + [vmem] + [hbm] * 3,
        out_specs=(vmem, vmem),
        scratch_shapes=[
            pltpu.VMEM(value_weight.shape, bf16),
            pltpu.VMEM((tok, chans), bf16),
            pltpu.VMEM((PLANE, tok, lanes), bf16),
            pltpu.VMEM((PLANE, tok, STATE), bf16),
            pltpu.VMEM((PLANE, tok, STATE), bf16),
            pltpu.VMEM((PLANE, heads, tok), f32),
            pltpu.VMEM((PLANE, tok, q_lanes), bf16),
            pltpu.VMEM((nz, PLANE, tok, HEAD_DIM), bf16),
            pltpu.VMEM((nz, PLANE, tok, HEAD_DIM), bf16),
            pltpu.VMEM((n_chunks, STATE, BLOCK), f32),
            pltpu.VMEM((n_chunks, STATE, BLOCK), f32),
            pltpu.VMEM((n_chunks, PLANE, tok, BLOCK), bf16),
            pltpu.VMEM((n_chunks, PLANE, tok, BLOCK), bf16),
            pltpu.VMEM((KVHEADS, tok, HEAD_DIM), bf16),
            pltpu.VMEM((n_tp, PLANE, tok, HEAD_DIM), bf16),
            pltpu.VMEM((nz, span, span), f32),
            pltpu.VMEM((nz, q_heads, span, span), bf16),
            pltpu.VMEM((q_heads, span, HEAD_DIM), f32),
            pltpu.VMEM((q_heads, span, HEAD_DIM), f32),
            pltpu.VMEM((q_heads, PLANE, tok, HEAD_DIM), bf16),
            pltpu.VMEM((n_blocks, n_chunks, BLOCK, BLOCK), f32),
            pltpu.VMEM((n_blocks, n_chunks, BLOCK, BLOCK), f32),
            pltpu.VMEM((tok, chans), f32),
            dma, dma, dma((6,)),
            dma((6, PLANE)), dma((6, PLANE)),
            dma((nz,)), dma((nz,)),
            dma((n_chunks,)), dma((n_chunks,)),
            dma((n_chunks, PLANE)), dma((n_chunks, PLANE)),
            dma((n_tp, PLANE)), dma((n_tp, PLANE)),
            dma((nz,)), dma((nz,)),
            dma((q_heads, PLANE)), dma((q_heads, PLANE)),
        ],
        compiler_params=pltpu.CompilerParams(
            collective_id=0, has_side_effects=True, vmem_limit_bytes=52 * 1024 * 1024
        ),
    )(
        mamba_x, gate_z, b_in, c_in,
        dt_raw.reshape(PLANE, heads, tok), a_log.reshape(1, -1),
        skip_d.reshape(1, -1), norm_gain.reshape(1, chans), value_weight, queries, keys,
    )


def solution(mesh):
    placed = (
        P("seq", "tp"),
        P("seq", "tp"),
        P("seq", "tp"),
        P("seq", "tp"),
        P("tp", "seq"),
        P("tp"),
        P("tp"),
        P("tp"),
        P("tp", None),
        P("seq", "tp"),
        P("seq", "tp"),
    )
    return jax.shard_map(
        functools.partial(per_device, mesh.shape["seq"], mesh.shape["tp"]),
        mesh=mesh,
        in_specs=placed,
        out_specs=(P("seq", "tp"), P("seq", "tp")),
        check_vma=False,
    )
```

```python
import functools
import math

import jax
import jax.numpy as jnp
from jax import lax
from jax.experimental import pallas as pl
from jax.experimental.pallas import tpu as pltpu
from jax.sharding import PartitionSpec as P

MHEAD_DIM = 64
STATE = 128
GROUP_HEADS = 16
QHEADS = 32
KVHEADS = 8
HEAD_DIM = 128
PLANE = 4
BLOCK = 128
NORM_EPS = 1e-05

MESH = pl.DeviceIdType.MESH
f32 = jnp.float32
bf16 = jnp.bfloat16


def dot(a, b, ca=1, cb=0):
    return lax.dot_general(a, b, (((ca,), (cb,)), ((), ())), preferred_element_type=f32)


def kernel(
    n_seq, n_tp,
    x_hbm, z_hbm, b_hbm, c_hbm, dt_hbm, alog_hbm, skip_hbm, gain_hbm, w_hbm, q_hbm, k_hbm,
    mo_ref, att_ref,
    w_ref, z_ref, xo, bo, co, dto, qo, ko, vo, sin, sout, yo, yh, part, vp, scores, probs, sums, accs, ao,
    grown, tail_w, silu, alog_ref, skip_ref, gain_ref,
    w_sem, z_sem, s_sem, own_sem, a_send, a_recv, k_send, k_recv, c_send, c_recv, y_send, y_recv,
    p_send, p_recv, v_send, v_recv, o_send, o_recv,
):
    tok, chans = x_hbm.shape
    lanes = chans // PLANE
    heads = lanes // MHEAD_DIM
    nz = n_seq // PLANE
    span = PLANE * tok
    kv_here = k_hbm.shape[1] // HEAD_DIM
    q_lanes = q_hbm.shape[1] // PLANE
    q_heads = q_lanes // HEAD_DIM
    groups = b_hbm.shape[1] // STATE
    seq = lax.axis_index("seq")
    t = lax.axis_index("tp")
    z = seq // PLANE
    p = seq % PLANE

    def seq_id(zz, pp):
        return zz * PLANE + pp

    def cols(index, width):
        return pl.ds(pl.multiple_of(index * width, width), width)

    barrier = pltpu.get_barrier_semaphore()
    for dt_ in range(n_tp):
        for dp in range(PLANE):
            if dt_ or dp:
                pl.semaphore_signal(
                    barrier, inc=1,
                    device_id=(seq_id(z, (p + dp) % PLANE), (t + dt_) % n_tp), device_id_type=MESH,
                )
    for dz in range(1, nz):
        pl.semaphore_signal(
            barrier, inc=1, device_id=(seq_id((z + dz) % nz, p), t), device_id_type=MESH
        )

    def pieces(to, slot):
        group = to * groups // PLANE
        kv = to * kv_here // PLANE
        return (
            (k_hbm.at[:, cols(kv, HEAD_DIM)], ko.at[z, slot]),
            (dt_hbm.at[to], dto.at[slot]),
            (b_hbm.at[:, cols(group, STATE)], bo.at[slot]),
            (x_hbm.at[:, cols(to, lanes)], xo.at[slot]),
            (c_hbm.at[:, cols(group, STATE)], co.at[slot]),
            (q_hbm.at[:, cols(to, q_lanes)], qo.at[slot]),
        )

    def exchange(d, i, src, dst):
        return pltpu.make_async_remote_copy(
            src_ref=src, dst_ref=dst, send_sem=a_send.at[i, d], recv_sem=a_recv.at[i, d],
            device_id=(seq_id(z, (p + d) % PLANE), t), device_id_type=MESH,
        )

    small = [
        pltpu.make_async_copy(alog_hbm, alog_ref, s_sem.at[0]),
        pltpu.make_async_copy(skip_hbm, skip_ref, s_sem.at[1]),
        pltpu.make_async_copy(gain_hbm, gain_ref, s_sem.at[2]),
    ]
    for copy in small:
        copy.start()
    sends = {}
    for i in range(6):
        src, dst = pieces(p, p)[i]
        sends[i, 0] = pltpu.make_async_copy(src, dst, own_sem.at[i])
        sends[i, 0].start()
    pl.semaphore_wait(barrier, n_tp * PLANE - 1 + nz - 1)
    for i in range(6):
        for d in range(1, PLANE):
            src, dst = pieces((p + d) % PLANE, p)[i]
            sends[i, d] = exchange(d, i, src, dst)
            sends[i, d].start()
    load_z = pltpu.make_async_copy(z_hbm, z_ref, z_sem)
    load_z.start()
    load_w = pltpu.make_async_copy(w_hbm, w_ref, w_sem)
    load_w.start()

    def arrived(i):
        for d in range(1, PLANE):
            src, dst = pieces(p, (p + PLANE - d) % PLANE)[i]
            exchange(d, i, src, dst).wait_recv()
        sends[i, 0].wait()

    def later(buffer, zz, send, recv):
        return pltpu.make_async_remote_copy(
            src_ref=buffer.at[z], dst_ref=buffer.at[z], send_sem=send.at[zz], recv_sem=recv.at[z],
            device_id=(seq_id(zz, p), t), device_id_type=MESH,
        )

    def earlier(buffer, zz, send, recv):
        return pltpu.make_async_remote_copy(
            src_ref=buffer.at[zz], dst_ref=buffer.at[zz], send_sem=send.at[zz], recv_sem=recv.at[zz],
            device_id=(seq_id(zz, p), t), device_id_type=MESH,
        )

    def push(buffer, send, recv):
        for zz in range(1, nz):
            @pl.when(zz > z)
            def _():
                later(buffer, zz, send, recv).start()

    def pushed(buffer, send, recv):
        for zz in range(1, nz):
            @pl.when(zz > z)
            def _():
                later(buffer, zz, send, recv).wait_send()

    for copy in small:
        copy.wait()
    arrived(0)
    push(ko, k_send, k_recv)

    arrived(1)
    per_block = BLOCK // tok
    n_blocks = span // BLOCK
    rows = n_blocks * heads
    head_row = lax.broadcasted_iota(jnp.int32, (heads, BLOCK), 0)
    log_rate = jnp.zeros((heads, BLOCK), f32)
    for h in range(heads):
        log_rate = jnp.where(head_row == h, alog_ref[0, p * heads + h], log_rate)
    raw = jnp.concatenate(
        [
            jnp.concatenate([dto[blk * per_block + j] for j in range(per_block)], axis=1)
            for blk in range(n_blocks)
        ],
        axis=0,
    )
    steps = jnp.maximum(raw, 0.0) + jnp.log1p(jnp.exp(-jnp.abs(raw)))
    log_step = -steps * jnp.concatenate([jnp.exp(log_rate)] * n_blocks, axis=0)
    row = lax.broadcasted_iota(jnp.int32, (BLOCK, BLOCK), 0)
    col = lax.broadcasted_iota(jnp.int32, (BLOCK, BLOCK), 1)
    causal = row >= col
    left_half = col < MHEAD_DIM
    upto = (row <= col).astype(bf16)
    first = log_step.astype(bf16).astype(f32)
    second = (log_step - first).astype(bf16).astype(f32)
    third = log_step - first - second
    summed = dot(jnp.concatenate([first, second, third], axis=0).astype(bf16), upto)
    l_rows = summed[:rows] + summed[rows : 2 * rows] + summed[2 * rows :]
    turned = jnp.concatenate([l_rows, steps, jnp.zeros((BLOCK - 2 * rows, BLOCK), f32)], axis=0).T

    def column(kind, blk, h):
        at = kind * rows + blk * heads + h
        return jnp.broadcast_to(turned[:, at : at + 1], (BLOCK, BLOCK))

    n_chunks = sin.shape[0]
    for blk in range(n_blocks):
        for i in range(n_chunks):
            l_both = jnp.where(left_half, column(0, blk, 2 * i), column(0, blk, 2 * i + 1))
            t_both = jnp.where(left_half, column(1, blk, 2 * i), column(1, blk, 2 * i + 1))
            grown[blk, i] = jnp.exp(l_both)
            tail_w[blk, i] = jnp.exp(l_both[BLOCK - 1 :, :] - l_both) * t_both

    def chain(i):
        return pltpu.make_async_remote_copy(
            src_ref=sout.at[i], dst_ref=sin.at[i], send_sem=c_send.at[i], recv_sem=c_recv.at[i],
            device_id=(seq_id((z + 1) % nz, p), t), device_id_type=MESH,
        )

    def chunk(i):
        return slice(i * BLOCK, (i + 1) * BLOCK)

    arrived(2)
    arrived(3)
    b_blocks = [
        bo[pl.ds(blk * per_block, per_block)].reshape(BLOCK, STATE) for blk in range(n_blocks)
    ]

    def x_block(blk, i):
        return xo[pl.ds(blk * per_block, per_block), :, chunk(i)].reshape(BLOCK, BLOCK)

    before = {}
    for i in range(n_chunks):
        dec, own = jnp.ones((1, BLOCK), f32), jnp.zeros((STATE, BLOCK), f32)
        for blk in range(n_blocks):
            before[blk, i] = (dec, own)
            weighted = (x_block(blk, i).astype(f32) * tail_w[blk, i]).astype(bf16)
            fade = grown[blk, i, BLOCK - 1 :, :]
            own = fade * own + dot(b_blocks[blk], weighted, 0, 0)
            dec = dec * fade
        before[n_blocks, i] = (dec, own)
        sout[i] = own

        @pl.when(z == 0)
        def _():
            chain(i).start()

    @pl.when(z == 0)
    def _():
        sin[...] = jnp.zeros_like(sin)

    arrived(4)
    c_blocks = [
        co[pl.ds(blk * per_block, per_block)].reshape(BLOCK, STATE) for blk in range(n_blocks)
    ]
    cross = [dot(c_blocks[blk], b_blocks[blk], 1, 1) for blk in range(n_blocks)]

    def give_back(i, d):
        return pltpu.make_async_remote_copy(
            src_ref=yo.at[i, (p + d) % PLANE], dst_ref=yh.at[i, p],
            send_sem=y_send.at[i, d], recv_sem=y_recv.at[i, d],
            device_id=(seq_id(z, (p + d) % PLANE), t), device_id_type=MESH,
        )

    within = (
        lax.broadcasted_iota(jnp.int32, (span, span), 0)
        >= lax.broadcasted_iota(jnp.int32, (span, span), 1)
    )
    score_scale = 1.0 / math.sqrt(HEAD_DIM)

    def attend(h):
        query = qo[:, :, h * HEAD_DIM : (h + 1) * HEAD_DIM].reshape(span, HEAD_DIM)
        own_scores = jnp.where(
            within, dot(query, ko[z].reshape(span, HEAD_DIM), 1, 1) * score_scale, -jnp.inf
        )

        def score(zz, largest):
            s = dot(query, ko[zz].reshape(span, HEAD_DIM), 1, 1) * score_scale
            scores[zz] = s
            return jnp.maximum(largest, jnp.max(s, axis=1, keepdims=True))

        largest = lax.fori_loop(0, z, score, jnp.max(own_scores, axis=1, keepdims=True))
        weights = jnp.exp(own_scores - largest)
        probs[z, h] = weights.astype(bf16)

        def weigh(zz, total):
            e = jnp.exp(scores[zz] - largest)
            probs[zz, h] = e.astype(bf16)
            return total + jnp.sum(e, axis=1, keepdims=True)

        total = lax.fori_loop(0, z, weigh, jnp.sum(weights, axis=1, keepdims=True))
        sums[h] = jnp.broadcast_to(total, (span, HEAD_DIM))

    attended = 0
    for i in range(n_chunks):
        @pl.when(z > 0)
        def _():
            chain(i).wait_recv()

            @pl.when(z < nz - 1)
            def _():
                dec, own = before[n_blocks, i]
                sout[i] = dec * sin[i] + sout[i]
                chain(i).start()

        skip = jnp.where(
            left_half, skip_ref[0, p * heads + 2 * i], skip_ref[0, p * heads + 2 * i + 1]
        )
        for blk in range(n_blocks):
            mixes = []
            for h in (2 * i, 2 * i + 1):
                at = blk * heads + h
                gaps = jnp.where(causal, column(0, blk, h) - l_rows[at : at + 1, :], -jnp.inf)
                mixes.append((cross[blk] * jnp.exp(gaps) * steps[at : at + 1, :]).astype(bf16))
            xb = x_block(blk, i)
            both = dot(jnp.concatenate(mixes, axis=0), xb)
            local = jnp.where(left_half, both[:BLOCK], both[BLOCK:])
            dec, own = before[blk, i]
            state = dec * sin[i] + own
            high = state.astype(bf16)
            low = (state - high.astype(f32)).astype(bf16)
            carried = dot(c_blocks[blk], high) + dot(c_blocks[blk], low)
            y = local + grown[blk, i] * carried + skip * xb.astype(f32)
            yo[i, pl.ds(blk * per_block, per_block)] = y.astype(bf16).reshape(
                per_block, tok, BLOCK
            )
        for d in range(1, PLANE):
            give_back(i, d).start()
        yh[i, p] = yo[i, p]
        while attended < q_heads and (attended + 1) * n_chunks <= (i + 1) * q_heads:
            if attended == 0:
                arrived(5)
                for zz in range(nz - 1):
                    @pl.when(zz < z)
                    def _():
                        earlier(ko, zz, k_send, k_recv).wait_recv()
            attend(attended)
            attended += 1

    load_z.wait()
    zg = z_ref[...].astype(f32)
    silu[...] = zg / (1.0 + jnp.exp(-zg))
    for i in range(n_chunks):
        for d in range(1, PLANE):
            give_back(i, d).wait_recv()
    group_lanes = chans // groups
    for g in range(groups):
        gc = slice(g * group_lanes, (g + 1) * group_lanes)
        owners = range(g * PLANE // groups, (g + 1) * PLANE // groups)
        ssm = jnp.concatenate([yh[i, j] for j in owners for i in range(n_chunks)], axis=1)
        gated = ssm.astype(f32) * silu[:, gc]
        inverse = lax.rsqrt(jnp.mean(gated * gated, axis=1, keepdims=True) + NORM_EPS)
        mo_ref[:, gc] = (gated * inverse * gain_ref[:, gc]).astype(bf16)

    def partial_copy(dt_, dp):
        tt, pp = (t + dt_) % n_tp, (p + dp) % PLANE
        return pltpu.make_async_remote_copy(
            src_ref=part.at[tt * kv_here + pp * kv_here // PLANE], dst_ref=vp.at[t, p],
            send_sem=p_send.at[dt_, dp], recv_sem=p_recv.at[dt_, dp],
            device_id=(seq_id(z, pp), tt), device_id_type=MESH,
        )

    offsets = [(dt_, dp) for dt_ in range(n_tp) for dp in range(PLANE) if dt_ or dp]
    load_w.wait()
    for n in range(w_ref.shape[1] // 256):
        product = dot(mo_ref[...], w_ref[:, n * 256 : (n + 1) * 256]).astype(bf16)
        part[2 * n] = product[:, :HEAD_DIM]
        part[2 * n + 1] = product[:, HEAD_DIM:]
        for dt_, dp in offsets:
            tt, pp = (t + dt_) % n_tp, (p + dp) % PLANE

            @pl.when((tt * kv_here + pp * kv_here // PLANE) // 2 == n)
            def _():
                partial_copy(dt_, dp).start()

    vp[t, p] = part[t * kv_here + p * kv_here // PLANE]
    accs[...] = jnp.zeros_like(accs)

    def take(zz):
        earlier(vo, zz, v_send, v_recv).wait_recv()
        for h in range(q_heads):
            accs[h] += dot(probs[zz, h], vo[zz].reshape(span, HEAD_DIM))

    for zz in range(nz - 2):
        @pl.when(zz < z - 1)
        def _():
            take(zz)

    for dt_, dp in offsets:
        partial_copy(dt_, dp).wait_recv()
    values = vp[0].astype(f32)
    for tt in range(1, n_tp):
        values = values + vp[tt].astype(f32)
    vo[z] = values.astype(bf16)
    push(vo, v_send, v_recv)

    for zz in range(nz - 1):
        @pl.when(zz == z - 1)
        def _():
            take(zz)

    def hand_out(h, d):
        return pltpu.make_async_remote_copy(
            src_ref=ao.at[h, (p + d) % PLANE], dst_ref=att_ref.at[:, cols(p * q_heads + h, HEAD_DIM)],
            send_sem=o_send.at[h, d], recv_sem=o_recv.at[h, d],
            device_id=(seq_id(z, (p + d) % PLANE), t), device_id_type=MESH,
        )

    for h in range(q_heads):
        acc = accs[h] + dot(probs[z, h], vo[z].reshape(span, HEAD_DIM))
        ao[h] = (acc / sums[h]).astype(bf16).reshape(PLANE, tok, HEAD_DIM)
        for d in range(1, PLANE):
            hand_out(h, d).start()
        att_ref[:, cols(p * q_heads + h, HEAD_DIM)] = ao[h, p]

    for i in range(6):
        for d in range(1, PLANE):
            sends[i, d].wait_send()

    @pl.when(z < nz - 1)
    def _():
        for i in range(n_chunks):
            chain(i).wait_send()

    for i in range(n_chunks):
        for d in range(1, PLANE):
            give_back(i, d).wait_send()
    pushed(ko, k_send, k_recv)
    pushed(vo, v_send, v_recv)
    for dt_, dp in offsets:
        partial_copy(dt_, dp).wait_send()
    for h in range(q_heads):
        for d in range(1, PLANE):
            hand_out(h, d).wait_recv()
            hand_out(h, d).wait_send()


def per_device(
    n_seq, n_tp,
    mamba_x, gate_z, b_in, c_in, dt_raw, a_log, skip_d, norm_gain, value_weight, queries, keys,
):
    tok, chans = mamba_x.shape
    lanes = chans // PLANE
    heads = lanes // MHEAD_DIM
    nz = n_seq // PLANE
    span = PLANE * tok
    q_lanes = queries.shape[1] // PLANE
    q_heads = q_lanes // HEAD_DIM
    n_chunks = lanes // BLOCK
    n_blocks = span // BLOCK
    vmem = pl.BlockSpec(memory_space=pltpu.VMEM)
    hbm = pl.BlockSpec(memory_space=pltpu.HBM)
    dma = pltpu.SemaphoreType.DMA
    return pl.pallas_call(
        functools.partial(kernel, n_seq, n_tp),
        out_shape=(
            jax.ShapeDtypeStruct((tok, chans), bf16),
            jax.ShapeDtypeStruct(queries.shape, bf16),
        ),
        in_specs=[hbm] * 11,
        out_specs=(vmem, vmem),
        scratch_shapes=[
            pltpu.VMEM(value_weight.shape, bf16),
            pltpu.VMEM((tok, chans), bf16),
            pltpu.VMEM((PLANE, tok, lanes), bf16),
            pltpu.VMEM((PLANE, tok, STATE), bf16),
            pltpu.VMEM((PLANE, tok, STATE), bf16),
            pltpu.VMEM((PLANE, heads, tok), f32),
            pltpu.VMEM((PLANE, tok, q_lanes), bf16),
            pltpu.VMEM((nz, PLANE, tok, HEAD_DIM), bf16),
            pltpu.VMEM((nz, PLANE, tok, HEAD_DIM), bf16),
            pltpu.VMEM((n_chunks, STATE, BLOCK), f32),
            pltpu.VMEM((n_chunks, STATE, BLOCK), f32),
            pltpu.VMEM((n_chunks, PLANE, tok, BLOCK), bf16),
            pltpu.VMEM((n_chunks, PLANE, tok, BLOCK), bf16),
            pltpu.VMEM((KVHEADS, tok, HEAD_DIM), bf16),
            pltpu.VMEM((n_tp, PLANE, tok, HEAD_DIM), bf16),
            pltpu.VMEM((nz, span, span), f32),
            pltpu.VMEM((nz, q_heads, span, span), bf16),
            pltpu.VMEM((q_heads, span, HEAD_DIM), f32),
            pltpu.VMEM((q_heads, span, HEAD_DIM), f32),
            pltpu.VMEM((q_heads, PLANE, tok, HEAD_DIM), bf16),
            pltpu.VMEM((n_blocks, n_chunks, BLOCK, BLOCK), f32),
            pltpu.VMEM((n_blocks, n_chunks, BLOCK, BLOCK), f32),
            pltpu.VMEM((tok, chans), f32),
            pltpu.SMEM((1, PLANE * heads), f32),
            pltpu.SMEM((1, PLANE * heads), f32),
            pltpu.VMEM((1, chans), f32),
            dma, dma, dma((3,)), dma((6,)),
            dma((6, PLANE)), dma((6, PLANE)),
            dma((nz,)), dma((nz,)),
            dma((n_chunks,)), dma((n_chunks,)),
            dma((n_chunks, PLANE)), dma((n_chunks, PLANE)),
            dma((n_tp, PLANE)), dma((n_tp, PLANE)),
            dma((nz,)), dma((nz,)),
            dma((q_heads, PLANE)), dma((q_heads, PLANE)),
        ],
        compiler_params=pltpu.CompilerParams(
            collective_id=0, has_side_effects=True, vmem_limit_bytes=62 * 1024 * 1024
        ),
    )(
        mamba_x, gate_z, b_in, c_in,
        dt_raw.reshape(PLANE, heads, tok), a_log.reshape(1, -1),
        skip_d.reshape(1, -1), norm_gain.reshape(1, chans), value_weight, queries, keys,
    )


def solution(mesh):
    placed = (
        P("seq", "tp"),
        P("seq", "tp"),
        P("seq", "tp"),
        P("seq", "tp"),
        P("tp", "seq"),
        P("tp"),
        P("tp"),
        P("tp"),
        P("tp", None),
        P("seq", "tp"),
        P("seq", "tp"),
    )
    return jax.shard_map(
        functools.partial(per_device, mesh.shape["seq"], mesh.shape["tp"]),
        mesh=mesh,
        in_specs=placed,
        out_specs=(P("seq", "tp"), P("seq", "tp")),
        check_vma=False,
    )
```

```python
import functools
import math

import jax
import jax.numpy as jnp
from jax import lax
from jax.experimental import pallas as pl
from jax.experimental.pallas import tpu as pltpu
from jax.sharding import PartitionSpec as P

MHEAD_DIM = 64
STATE = 128
GROUP_HEADS = 16
QHEADS = 32
KVHEADS = 8
HEAD_DIM = 128
PLANE = 4
BLOCK = 128
NORM_EPS = 1e-05

MESH = pl.DeviceIdType.MESH
f32 = jnp.float32
bf16 = jnp.bfloat16


def dot(a, b, ca=1, cb=0):
    return lax.dot_general(a, b, (((ca,), (cb,)), ((), ())), preferred_element_type=f32)


def kernel(
    n_seq, n_tp,
    x_hbm, z_hbm, b_hbm, c_hbm, dt_hbm, alog_hbm, skip_hbm, gain_hbm, w_hbm, q_hbm, k_hbm,
    mo_hbm, att_hbm,
    w_ref, z_ref, xo, bo, co, dto, qo, ko, vo, sin, sout, yo, yh, part, vp, scores, probs, sums, accs, ao,
    grown, silu, mo_ref, alog_ref, skip_ref, gain_ref,
    w_sem, z_sem, m_sem, s_sem, own_sem, a_send, a_recv, k_send, k_recv, c_send, c_recv, y_send, y_recv,
    p_send, p_recv, v_send, v_recv, o_send, o_recv, f_sem,
):
    tok, chans = x_hbm.shape
    lanes = chans // PLANE
    heads = lanes // MHEAD_DIM
    nz = n_seq // PLANE
    span = PLANE * tok
    kv_here = k_hbm.shape[1] // HEAD_DIM
    q_lanes = q_hbm.shape[1] // PLANE
    q_heads = q_lanes // HEAD_DIM
    groups = b_hbm.shape[1] // STATE
    n_chunks = lanes // BLOCK
    order = [0, 1, 2, 5, 3] + list(range(6, 5 + n_chunks)) + [4]
    seq = lax.axis_index("seq")
    t = lax.axis_index("tp")
    z = seq // PLANE
    p = seq % PLANE

    def seq_id(zz, pp):
        return zz * PLANE + pp

    def cols(index, width):
        return pl.ds(pl.multiple_of(index * width, width), width)

    barrier = pltpu.get_barrier_semaphore()
    for dt_ in range(n_tp):
        for dp in range(PLANE):
            if dt_ or dp:
                pl.semaphore_signal(
                    barrier, inc=1,
                    device_id=(seq_id(z, (p + dp) % PLANE), (t + dt_) % n_tp), device_id_type=MESH,
                )
    for dz in range(1, nz):
        pl.semaphore_signal(
            barrier, inc=1, device_id=(seq_id((z + dz) % nz, p), t), device_id_type=MESH
        )

    def pieces(to, slot):
        group = to * groups // PLANE
        kv = to * kv_here // PLANE
        return (
            (k_hbm.at[:, cols(kv, HEAD_DIM)], ko.at[z, slot]),
            (dt_hbm.at[to], dto.at[slot]),
            (b_hbm.at[:, cols(group, STATE)], bo.at[slot]),
            (c_hbm.at[:, cols(group, STATE)], co.at[slot]),
            (q_hbm.at[:, cols(to, q_lanes)], qo.at[slot]),
        ) + tuple(
            (x_hbm.at[:, cols(to * n_chunks + i, BLOCK)], xo.at[i, slot]) for i in range(n_chunks)
        )

    def exchange(d, i, src, dst):
        return pltpu.make_async_remote_copy(
            src_ref=src, dst_ref=dst, send_sem=a_send.at[i, d], recv_sem=a_recv.at[i, d],
            device_id=(seq_id(z, (p + d) % PLANE), t), device_id_type=MESH,
        )

    small = [
        pltpu.make_async_copy(alog_hbm, alog_ref, s_sem.at[0]),
        pltpu.make_async_copy(skip_hbm, skip_ref, s_sem.at[1]),
        pltpu.make_async_copy(gain_hbm, gain_ref, s_sem.at[2]),
    ]
    for copy in small:
        copy.start()
    sends = {}
    for i in order:
        src, dst = pieces(p, p)[i]
        sends[i, 0] = pltpu.make_async_copy(src, dst, own_sem.at[i])
        sends[i, 0].start()
    pl.semaphore_wait(barrier, n_tp * PLANE - 1 + nz - 1)
    for i in order:
        for d in range(1, PLANE):
            src, dst = pieces((p + d) % PLANE, p)[i]
            sends[i, d] = exchange(d, i, src, dst)
            sends[i, d].start()
    load_z = pltpu.make_async_copy(z_hbm, z_ref, z_sem)
    load_z.start()
    load_w = pltpu.make_async_copy(w_hbm, w_ref, w_sem)
    load_w.start()

    def arrived(i):
        for d in range(1, PLANE):
            src, dst = pieces(p, (p + PLANE - d) % PLANE)[i]
            exchange(d, i, src, dst).wait_recv()
        sends[i, 0].wait()

    def later(buffer, zz, send, recv):
        return pltpu.make_async_remote_copy(
            src_ref=buffer.at[z], dst_ref=buffer.at[z], send_sem=send.at[zz], recv_sem=recv.at[z],
            device_id=(seq_id(zz, p), t), device_id_type=MESH,
        )

    def earlier(buffer, zz, send, recv):
        return pltpu.make_async_remote_copy(
            src_ref=buffer.at[zz], dst_ref=buffer.at[zz], send_sem=send.at[zz], recv_sem=recv.at[zz],
            device_id=(seq_id(zz, p), t), device_id_type=MESH,
        )

    def push(buffer, send, recv):
        for zz in range(1, nz):
            @pl.when(zz > z)
            def _():
                later(buffer, zz, send, recv).start()

    def pushed(buffer, send, recv):
        for zz in range(1, nz):
            @pl.when(zz > z)
            def _():
                later(buffer, zz, send, recv).wait_send()

    for copy in small:
        copy.wait()
    arrived(0)
    push(ko, k_send, k_recv)

    arrived(1)
    per_block = BLOCK // tok
    n_blocks = span // BLOCK
    rows = n_blocks * heads
    head_row = lax.broadcasted_iota(jnp.int32, (heads, BLOCK), 0)
    log_rate = jnp.zeros((heads, BLOCK), f32)
    for h in range(heads):
        log_rate = jnp.where(head_row == h, alog_ref[0, p * heads + h], log_rate)
    raw = jnp.concatenate(
        [
            jnp.concatenate([dto[blk * per_block + j] for j in range(per_block)], axis=1)
            for blk in range(n_blocks)
        ],
        axis=0,
    )
    steps = jnp.maximum(raw, 0.0) + jnp.log1p(jnp.exp(-jnp.abs(raw)))
    log_step = -steps * jnp.concatenate([jnp.exp(log_rate)] * n_blocks, axis=0)
    row = lax.broadcasted_iota(jnp.int32, (BLOCK, BLOCK), 0)
    col = lax.broadcasted_iota(jnp.int32, (BLOCK, BLOCK), 1)
    causal = row >= col
    left_half = col < MHEAD_DIM
    upto = (row <= col).astype(bf16)
    first = log_step.astype(bf16).astype(f32)
    second = (log_step - first).astype(bf16).astype(f32)
    third = log_step - first - second
    summed = dot(jnp.concatenate([first, second, third], axis=0).astype(bf16), upto)
    l_rows = summed[:rows] + summed[rows : 2 * rows] + summed[2 * rows :]
    turned = jnp.concatenate([l_rows, steps, jnp.zeros((BLOCK - 2 * rows, BLOCK), f32)], axis=0).T

    def column(kind, blk, h):
        at = kind * rows + blk * heads + h
        return jnp.broadcast_to(turned[:, at : at + 1], (BLOCK, BLOCK))

    def chain(i):
        return pltpu.make_async_remote_copy(
            src_ref=sout.at[i], dst_ref=sin.at[i], send_sem=c_send.at[i], recv_sem=c_recv.at[i],
            device_id=(seq_id((z + 1) % nz, p), t), device_id_type=MESH,
        )

    def chunk(i):
        return slice(i * BLOCK, (i + 1) * BLOCK)

    arrived(2)
    b_blocks = [
        bo[pl.ds(blk * per_block, per_block)].reshape(BLOCK, STATE) for blk in range(n_blocks)
    ]

    def x_block(blk, i):
        return xo[i, pl.ds(blk * per_block, per_block)].reshape(BLOCK, BLOCK)

    before = {}

    def summarize(i):
        arrived(5 + i)
        dec, own = jnp.ones((1, BLOCK), f32), jnp.zeros((STATE, BLOCK), f32)
        for blk in range(n_blocks):
            before[blk, i] = (dec, own)
            l_both = jnp.where(left_half, column(0, blk, 2 * i), column(0, blk, 2 * i + 1))
            t_both = jnp.where(left_half, column(1, blk, 2 * i), column(1, blk, 2 * i + 1))
            growth = jnp.exp(l_both)
            grown[blk, i] = growth
            tail = jnp.exp(l_both[BLOCK - 1 :, :] - l_both) * t_both
            weighted = (x_block(blk, i).astype(f32) * tail).astype(bf16)
            fade = growth[BLOCK - 1 :, :]
            own = fade * own + dot(b_blocks[blk], weighted, 0, 0)
            dec = dec * fade
        before[n_blocks, i] = dec
        sout[i] = own

        @pl.when(z == 0)
        def _():
            chain(i).start()

    @pl.when(z == 0)
    def _():
        sin[...] = jnp.zeros_like(sin)

    def give_back(i, d):
        return pltpu.make_async_remote_copy(
            src_ref=yo.at[i, (p + d) % PLANE], dst_ref=yh.at[i, p],
            send_sem=y_send.at[i, d], recv_sem=y_recv.at[i, d],
            device_id=(seq_id(z, (p + d) % PLANE), t), device_id_type=MESH,
        )

    within = (
        lax.broadcasted_iota(jnp.int32, (span, span), 0)
        >= lax.broadcasted_iota(jnp.int32, (span, span), 1)
    )
    score_scale = 1.0 / math.sqrt(HEAD_DIM)

    def attend(h):
        query = qo[:, :, h * HEAD_DIM : (h + 1) * HEAD_DIM].reshape(span, HEAD_DIM)
        own_scores = jnp.where(
            within, dot(query, ko[z].reshape(span, HEAD_DIM), 1, 1) * score_scale, -jnp.inf
        )

        def score(zz, largest):
            s = dot(query, ko[zz].reshape(span, HEAD_DIM), 1, 1) * score_scale
            scores[zz] = s
            return jnp.maximum(largest, jnp.max(s, axis=1, keepdims=True))

        largest = lax.fori_loop(0, z, score, jnp.max(own_scores, axis=1, keepdims=True))
        weights = jnp.exp(own_scores - largest)
        probs[z, h] = weights.astype(bf16)

        def weigh(zz, total):
            e = jnp.exp(scores[zz] - largest)
            probs[zz, h] = e.astype(bf16)
            return total + jnp.sum(e, axis=1, keepdims=True)

        total = lax.fori_loop(0, z, weigh, jnp.sum(weights, axis=1, keepdims=True))
        sums[h] = jnp.broadcast_to(total, (span, HEAD_DIM))

    def attend_some(j, first_j, n_js, here):
        heads_now = [h for h in range(q_heads) if first_j + h * n_js // q_heads == j]
        if heads_now:
            @pl.when(here)
            def _():
                if heads_now[0] == 0:
                    arrived(4)
                    for zz in range(nz - 1):
                        @pl.when(zz < z)
                        def _():
                            earlier(ko, zz, k_send, k_recv).wait_recv()
                for h in heads_now:
                    attend(h)

    def finish(i):
        @pl.when(z > 0)
        def _():
            chain(i).wait_recv()

            @pl.when(z < nz - 1)
            def _():
                sout[i] = before[n_blocks, i] * sin[i] + sout[i]
                chain(i).start()

        skip = jnp.where(
            left_half, skip_ref[0, p * heads + 2 * i], skip_ref[0, p * heads + 2 * i + 1]
        )
        for blk in range(n_blocks):
            mixes = []
            for h in (2 * i, 2 * i + 1):
                at = blk * heads + h
                gaps = jnp.where(causal, column(0, blk, h) - l_rows[at : at + 1, :], -jnp.inf)
                mixes.append((cross[blk] * jnp.exp(gaps) * steps[at : at + 1, :]).astype(bf16))
            xb = x_block(blk, i)
            both = dot(jnp.concatenate(mixes, axis=0), xb)
            local = jnp.where(left_half, both[:BLOCK], both[BLOCK:])
            dec, own = before[blk, i]
            state = dec * sin[i] + own
            high = state.astype(bf16)
            low = (state - high.astype(f32)).astype(bf16)
            carried = dot(c_blocks[blk], high) + dot(c_blocks[blk], low)
            y = local + grown[blk, i] * carried + skip * xb.astype(f32)
            yo[i, pl.ds(blk * per_block, per_block)] = y.astype(bf16).reshape(
                per_block, tok, BLOCK
            )
        for d in range(1, PLANE):
            give_back(i, d).start()
        yh[i, p] = yo[i, p]

    half = n_chunks // 2
    for i in range(n_chunks + 3):
        if i < n_chunks:
            summarize(i)
        j = i - 3
        if j >= 0:
            if j == 0:
                arrived(3)
                c_blocks = [
                    co[pl.ds(blk * per_block, per_block)].reshape(BLOCK, STATE)
                    for blk in range(n_blocks)
                ]
                cross = [dot(c_blocks[blk], b_blocks[blk], 1, 1) for blk in range(n_blocks)]
            finish(j)
            attend_some(j, 0, half, z == nz - 1)
            attend_some(j, half, half, z < nz - 1)

    load_z.wait()
    zg = z_ref[...].astype(f32)
    silu[...] = zg / (1.0 + jnp.exp(-zg))
    for i in range(n_chunks):
        for d in range(1, PLANE):
            give_back(i, d).wait_recv()
    group_lanes = chans // groups
    for g in range(groups):
        gc = slice(g * group_lanes, (g + 1) * group_lanes)
        owners = range(g * PLANE // groups, (g + 1) * PLANE // groups)
        ssm = jnp.concatenate([yh[i, j] for j in owners for i in range(n_chunks)], axis=1)
        gated = ssm.astype(f32) * silu[:, gc]
        inverse = lax.rsqrt(jnp.mean(gated * gated, axis=1, keepdims=True) + NORM_EPS)
        mo_ref[:, gc] = (gated * inverse * gain_ref[:, gc]).astype(bf16)

    store = pltpu.make_async_copy(mo_ref, mo_hbm, m_sem)
    store.start()

    def partial_copy(dt_, dp):
        tt, pp = (t + dt_) % n_tp, (p + dp) % PLANE
        return pltpu.make_async_remote_copy(
            src_ref=part.at[tt * kv_here + pp * kv_here // PLANE], dst_ref=vp.at[t, p],
            send_sem=p_send.at[dt_, dp], recv_sem=p_recv.at[dt_, dp],
            device_id=(seq_id(z, pp), tt), device_id_type=MESH,
        )

    offsets = [(dt_, dp) for dt_ in range(n_tp) for dp in range(PLANE) if dt_ or dp]
    load_w.wait()
    for n in range(w_ref.shape[1] // 256):
        product = dot(mo_ref[...], w_ref[:, n * 256 : (n + 1) * 256]).astype(bf16)
        part[2 * n] = product[:, :HEAD_DIM]
        part[2 * n + 1] = product[:, HEAD_DIM:]
        for dt_, dp in offsets:
            tt, pp = (t + dt_) % n_tp, (p + dp) % PLANE

            @pl.when((tt * kv_here + pp * kv_here // PLANE) // 2 == n)
            def _():
                partial_copy(dt_, dp).start()

    vp[t, p] = part[t * kv_here + p * kv_here // PLANE]
    accs[...] = jnp.zeros_like(accs)

    def take(zz):
        earlier(vo, zz, v_send, v_recv).wait_recv()
        for h in range(q_heads):
            accs[h] += dot(probs[zz, h], vo[zz].reshape(span, HEAD_DIM))

    for zz in range(nz - 2):
        @pl.when(zz < z - 1)
        def _():
            take(zz)

    for dt_, dp in offsets:
        partial_copy(dt_, dp).wait_recv()
    values = vp[0].astype(f32)
    for tt in range(1, n_tp):
        values = values + vp[tt].astype(f32)
    vo[z] = values.astype(bf16)
    push(vo, v_send, v_recv)

    for zz in range(nz - 1):
        @pl.when(zz == z - 1)
        def _():
            take(zz)

    def hand_out(h, d):
        return pltpu.make_async_remote_copy(
            src_ref=ao.at[h, (p + d) % PLANE], dst_ref=att_hbm.at[:, cols(p * q_heads + h, HEAD_DIM)],
            send_sem=o_send.at[h, d], recv_sem=o_recv.at[h, d],
            device_id=(seq_id(z, (p + d) % PLANE), t), device_id_type=MESH,
        )

    mine = []
    for h in range(q_heads):
        acc = accs[h] + dot(probs[z, h], vo[z].reshape(span, HEAD_DIM))
        ao[h] = (acc / sums[h]).astype(bf16).reshape(PLANE, tok, HEAD_DIM)
        for d in range(1, PLANE):
            hand_out(h, d).start()
        mine.append(
            pltpu.make_async_copy(
                ao.at[h, p], att_hbm.at[:, cols(p * q_heads + h, HEAD_DIM)], f_sem.at[h]
            )
        )
        mine[-1].start()

    for i in order:
        for d in range(1, PLANE):
            sends[i, d].wait_send()

    @pl.when(z < nz - 1)
    def _():
        for i in range(n_chunks):
            chain(i).wait_send()

    for i in range(n_chunks):
        for d in range(1, PLANE):
            give_back(i, d).wait_send()
    pushed(ko, k_send, k_recv)
    pushed(vo, v_send, v_recv)
    for dt_, dp in offsets:
        partial_copy(dt_, dp).wait_send()
    store.wait()
    for h in range(q_heads):
        mine[h].wait()
        for d in range(1, PLANE):
            hand_out(h, d).wait_recv()
            hand_out(h, d).wait_send()


def copy_out(mo_in, att_in, mo_out, att_out, sem):
    first = pltpu.make_async_copy(mo_in, mo_out, sem.at[0])
    second = pltpu.make_async_copy(att_in, att_out, sem.at[1])
    first.start()
    second.start()
    first.wait()
    second.wait()


def per_device(
    n_seq, n_tp,
    mamba_x, gate_z, b_in, c_in, dt_raw, a_log, skip_d, norm_gain, value_weight, queries, keys,
):
    tok, chans = mamba_x.shape
    lanes = chans // PLANE
    heads = lanes // MHEAD_DIM
    nz = n_seq // PLANE
    span = PLANE * tok
    q_lanes = queries.shape[1] // PLANE
    q_heads = q_lanes // HEAD_DIM
    n_chunks = lanes // BLOCK
    n_blocks = span // BLOCK
    hbm = pl.BlockSpec(memory_space=pltpu.HBM)
    dma = pltpu.SemaphoreType.DMA
    results = pl.pallas_call(
        functools.partial(kernel, n_seq, n_tp),
        out_shape=(
            jax.ShapeDtypeStruct((tok, chans), bf16),
            jax.ShapeDtypeStruct(queries.shape, bf16),
        ),
        in_specs=[hbm] * 11,
        out_specs=(hbm, hbm),
        scratch_shapes=[
            pltpu.VMEM(value_weight.shape, bf16),
            pltpu.VMEM((tok, chans), bf16),
            pltpu.VMEM((n_chunks, PLANE, tok, BLOCK), bf16),
            pltpu.VMEM((PLANE, tok, STATE), bf16),
            pltpu.VMEM((PLANE, tok, STATE), bf16),
            pltpu.VMEM((PLANE, heads, tok), f32),
            pltpu.VMEM((PLANE, tok, q_lanes), bf16),
            pltpu.VMEM((nz, PLANE, tok, HEAD_DIM), bf16),
            pltpu.VMEM((nz, PLANE, tok, HEAD_DIM), bf16),
            pltpu.VMEM((n_chunks, STATE, BLOCK), f32),
            pltpu.VMEM((n_chunks, STATE, BLOCK), f32),
            pltpu.VMEM((n_chunks, PLANE, tok, BLOCK), bf16),
            pltpu.VMEM((n_chunks, PLANE, tok, BLOCK), bf16),
            pltpu.VMEM((KVHEADS, tok, HEAD_DIM), bf16),
            pltpu.VMEM((n_tp, PLANE, tok, HEAD_DIM), bf16),
            pltpu.VMEM((nz, span, span), f32),
            pltpu.VMEM((nz, q_heads, span, span), bf16),
            pltpu.VMEM((q_heads, span, HEAD_DIM), f32),
            pltpu.VMEM((q_heads, span, HEAD_DIM), f32),
            pltpu.VMEM((q_heads, PLANE, tok, HEAD_DIM), bf16),
            pltpu.VMEM((n_blocks, n_chunks, BLOCK, BLOCK), f32),
            pltpu.VMEM((tok, chans), f32),
            pltpu.VMEM((tok, chans), bf16),
            pltpu.SMEM((1, PLANE * heads), f32),
            pltpu.SMEM((1, PLANE * heads), f32),
            pltpu.VMEM((1, chans), f32),
            dma, dma, dma, dma((3,)), dma((5 + n_chunks,)),
            dma((5 + n_chunks, PLANE)), dma((5 + n_chunks, PLANE)),
            dma((nz,)), dma((nz,)),
            dma((n_chunks,)), dma((n_chunks,)),
            dma((n_chunks, PLANE)), dma((n_chunks, PLANE)),
            dma((n_tp, PLANE)), dma((n_tp, PLANE)),
            dma((nz,)), dma((nz,)),
            dma((q_heads, PLANE)), dma((q_heads, PLANE)), dma((q_heads,)),
        ],
        compiler_params=pltpu.CompilerParams(
            collective_id=0, has_side_effects=True, vmem_limit_bytes=62 * 1024 * 1024
        ),
    )(
        mamba_x, gate_z, b_in, c_in,
        dt_raw.reshape(PLANE, heads, tok), a_log.reshape(1, -1),
        skip_d.reshape(1, -1), norm_gain.reshape(1, chans), value_weight, queries, keys,
    )
    return pl.pallas_call(
        copy_out,
        out_shape=[jax.ShapeDtypeStruct(r.shape, r.dtype) for r in results],
        in_specs=[hbm] * 2,
        out_specs=[hbm] * 2,
        scratch_shapes=[dma((2,))],
        compiler_params=pltpu.CompilerParams(vmem_limit_bytes=62 * 1024 * 1024),
    )(*results)


def solution(mesh):
    placed = (
        P("seq", "tp"),
        P("seq", "tp"),
        P("seq", "tp"),
        P("seq", "tp"),
        P("tp", "seq"),
        P("tp"),
        P("tp"),
        P("tp"),
        P("tp", None),
        P("seq", "tp"),
        P("seq", "tp"),
    )
    return jax.shard_map(
        functools.partial(per_device, mesh.shape["seq"], mesh.shape["tp"]),
        mesh=mesh,
        in_specs=placed,
        out_specs=(P("seq", "tp"), P("seq", "tp")),
        check_vma=False,
    )
```

```python
import functools
import math

import jax
import jax.numpy as jnp
from jax import lax
from jax.experimental import pallas as pl
from jax.experimental.pallas import tpu as pltpu
from jax.sharding import PartitionSpec as P

MHEAD_DIM = 64
STATE = 128
GROUP_HEADS = 16
QHEADS = 32
KVHEADS = 8
HEAD_DIM = 128
PLANE = 4
BLOCK = 128
NORM_EPS = 1e-05

MESH = pl.DeviceIdType.MESH
f32 = jnp.float32
bf16 = jnp.bfloat16


def dot(a, b, ca=1, cb=0):
    return lax.dot_general(a, b, (((ca,), (cb,)), ((), ())), preferred_element_type=f32)


def kernel(
    n_seq, n_tp,
    x_hbm, z_hbm, b_hbm, c_hbm, dt_hbm, alog_hbm, skip_hbm, gain_hbm, w_hbm, q_hbm, k_hbm,
    mo_hbm, att_hbm,
    w_ref, z_ref, xo, bo, co, dto, qo, ko, vo, sin, sout, yo, yh, part, vp, scores, probs, sums, accs, ao,
    grown, silu, mo_ref, alog_ref, skip_ref, gain_ref,
    w_sem, z_sem, m_sem, s_sem, own_sem, a_send, a_recv, k_send, k_recv, c_send, c_recv, y_send, y_recv,
    p_send, p_recv, v_send, v_recv, o_send, o_recv, f_sem,
):
    tok, chans = x_hbm.shape
    lanes = chans // PLANE
    heads = lanes // MHEAD_DIM
    nz = n_seq // PLANE
    span = PLANE * tok
    kv_here = k_hbm.shape[1] // HEAD_DIM
    q_lanes = q_hbm.shape[1] // PLANE
    q_heads = q_lanes // HEAD_DIM
    groups = b_hbm.shape[1] // STATE
    n_chunks = lanes // BLOCK
    order = [0, 1, 2, 5, 3] + list(range(6, 5 + n_chunks)) + [4]
    seq = lax.axis_index("seq")
    t = lax.axis_index("tp")
    z = seq // PLANE
    p = seq % PLANE

    def seq_id(zz, pp):
        return zz * PLANE + pp

    def cols(index, width):
        return pl.ds(pl.multiple_of(index * width, width), width)

    barrier = pltpu.get_barrier_semaphore()
    for dt_ in range(n_tp):
        for dp in range(PLANE):
            if dt_ or dp:
                pl.semaphore_signal(
                    barrier, inc=1,
                    device_id=(seq_id(z, (p + dp) % PLANE), (t + dt_) % n_tp), device_id_type=MESH,
                )
    for dz in range(1, nz):
        pl.semaphore_signal(
            barrier, inc=1, device_id=(seq_id((z + dz) % nz, p), t), device_id_type=MESH
        )

    def pieces(to, slot):
        group = to * groups // PLANE
        kv = to * kv_here // PLANE
        return (
            (k_hbm.at[:, cols(kv, HEAD_DIM)], ko.at[z, slot]),
            (dt_hbm.at[to], dto.at[slot]),
            (b_hbm.at[:, cols(group, STATE)], bo.at[slot]),
            (c_hbm.at[:, cols(group, STATE)], co.at[slot]),
            (q_hbm.at[:, cols(to, q_lanes)], qo.at[slot]),
        ) + tuple(
            (x_hbm.at[:, cols(to * n_chunks + i, BLOCK)], xo.at[i, slot]) for i in range(n_chunks)
        )

    def exchange(d, i, src, dst):
        return pltpu.make_async_remote_copy(
            src_ref=src, dst_ref=dst, send_sem=a_send.at[i, d], recv_sem=a_recv.at[i, d],
            device_id=(seq_id(z, (p + d) % PLANE), t), device_id_type=MESH,
        )

    small = [
        pltpu.make_async_copy(alog_hbm, alog_ref, s_sem.at[0]),
        pltpu.make_async_copy(skip_hbm, skip_ref, s_sem.at[1]),
        pltpu.make_async_copy(gain_hbm, gain_ref, s_sem.at[2]),
    ]
    for copy in small:
        copy.start()
    sends = {}
    for i in order:
        src, dst = pieces(p, p)[i]
        sends[i, 0] = pltpu.make_async_copy(src, dst, own_sem.at[i])
        sends[i, 0].start()
    pl.semaphore_wait(barrier, n_tp * PLANE - 1 + nz - 1)
    for i in order:
        for d in range(1, PLANE):
            src, dst = pieces((p + d) % PLANE, p)[i]
            sends[i, d] = exchange(d, i, src, dst)
            sends[i, d].start()
    load_z = pltpu.make_async_copy(z_hbm, z_ref, z_sem)
    load_z.start()
    load_w = pltpu.make_async_copy(w_hbm, w_ref, w_sem)
    load_w.start()

    def arrived(i):
        for d in range(1, PLANE):
            src, dst = pieces(p, (p + PLANE - d) % PLANE)[i]
            exchange(d, i, src, dst).wait_recv()
        sends[i, 0].wait()

    def later(buffer, zz, send, recv):
        return pltpu.make_async_remote_copy(
            src_ref=buffer.at[z], dst_ref=buffer.at[z], send_sem=send.at[zz], recv_sem=recv.at[z],
            device_id=(seq_id(zz, p), t), device_id_type=MESH,
        )

    def earlier(buffer, zz, send, recv):
        return pltpu.make_async_remote_copy(
            src_ref=buffer.at[zz], dst_ref=buffer.at[zz], send_sem=send.at[zz], recv_sem=recv.at[zz],
            device_id=(seq_id(zz, p), t), device_id_type=MESH,
        )

    def push(buffer, send, recv):
        for zz in range(1, nz):
            @pl.when(zz > z)
            def _():
                later(buffer, zz, send, recv).start()

    def pushed(buffer, send, recv):
        for zz in range(1, nz):
            @pl.when(zz > z)
            def _():
                later(buffer, zz, send, recv).wait_send()

    for copy in small:
        copy.wait()
    arrived(0)
    push(ko, k_send, k_recv)

    arrived(1)
    per_block = BLOCK // tok
    n_blocks = span // BLOCK
    rows = n_blocks * heads
    head_row = lax.broadcasted_iota(jnp.int32, (heads, BLOCK), 0)
    log_rate = jnp.zeros((heads, BLOCK), f32)
    for h in range(heads):
        log_rate = jnp.where(head_row == h, alog_ref[0, p * heads + h], log_rate)
    raw = jnp.concatenate(
        [
            jnp.concatenate([dto[blk * per_block + j] for j in range(per_block)], axis=1)
            for blk in range(n_blocks)
        ],
        axis=0,
    )
    steps = jnp.maximum(raw, 0.0) + jnp.log1p(jnp.exp(-jnp.abs(raw)))
    log_step = -steps * jnp.concatenate([jnp.exp(log_rate)] * n_blocks, axis=0)
    row = lax.broadcasted_iota(jnp.int32, (BLOCK, BLOCK), 0)
    col = lax.broadcasted_iota(jnp.int32, (BLOCK, BLOCK), 1)
    causal = row >= col
    left_half = col < MHEAD_DIM
    upto = (row <= col).astype(bf16)
    first = log_step.astype(bf16).astype(f32)
    second = (log_step - first).astype(bf16).astype(f32)
    third = log_step - first - second
    summed = dot(jnp.concatenate([first, second, third], axis=0).astype(bf16), upto)
    l_rows = summed[:rows] + summed[rows : 2 * rows] + summed[2 * rows :]
    turned = jnp.concatenate([l_rows, steps, jnp.zeros((BLOCK - 2 * rows, BLOCK), f32)], axis=0).T

    def column(kind, blk, h):
        at = kind * rows + blk * heads + h
        return jnp.broadcast_to(turned[:, at : at + 1], (BLOCK, BLOCK))

    def chain(i):
        return pltpu.make_async_remote_copy(
            src_ref=sout.at[i], dst_ref=sin.at[i], send_sem=c_send.at[i], recv_sem=c_recv.at[i],
            device_id=(seq_id((z + 1) % nz, p), t), device_id_type=MESH,
        )

    def chunk(i):
        return slice(i * BLOCK, (i + 1) * BLOCK)

    arrived(2)
    b_blocks = [
        bo[pl.ds(blk * per_block, per_block)].reshape(BLOCK, STATE) for blk in range(n_blocks)
    ]

    def x_block(blk, i):
        return xo[i, pl.ds(blk * per_block, per_block)].reshape(BLOCK, BLOCK)

    before = {}

    def summarize(i):
        arrived(5 + i)
        dec, own = jnp.ones((1, BLOCK), f32), jnp.zeros((STATE, BLOCK), f32)
        for blk in range(n_blocks):
            before[blk, i] = (dec, own)
            l_both = jnp.where(left_half, column(0, blk, 2 * i), column(0, blk, 2 * i + 1))
            t_both = jnp.where(left_half, column(1, blk, 2 * i), column(1, blk, 2 * i + 1))
            growth = jnp.exp(l_both)
            grown[blk, i] = growth
            tail = jnp.exp(l_both[BLOCK - 1 :, :] - l_both) * t_both
            weighted = (x_block(blk, i).astype(f32) * tail).astype(bf16)
            fade = growth[BLOCK - 1 :, :]
            own = fade * own + dot(b_blocks[blk], weighted, 0, 0)
            dec = dec * fade
        before[n_blocks, i] = dec
        sout[i] = own

        @pl.when(z == 0)
        def _():
            chain(i).start()

    @pl.when(z == 0)
    def _():
        sin[...] = jnp.zeros_like(sin)

    def give_back(i, d):
        return pltpu.make_async_remote_copy(
            src_ref=yo.at[i, (p + d) % PLANE], dst_ref=yh.at[i, p],
            send_sem=y_send.at[i, d], recv_sem=y_recv.at[i, d],
            device_id=(seq_id(z, (p + d) % PLANE), t), device_id_type=MESH,
        )

    within = (
        lax.broadcasted_iota(jnp.int32, (span, span), 0)
        >= lax.broadcasted_iota(jnp.int32, (span, span), 1)
    )
    score_scale = 1.0 / math.sqrt(HEAD_DIM)

    def attend(h):
        query = qo[:, :, h * HEAD_DIM : (h + 1) * HEAD_DIM].reshape(span, HEAD_DIM)
        own_scores = jnp.where(
            within, dot(query, ko[z].reshape(span, HEAD_DIM), 1, 1) * score_scale, -jnp.inf
        )

        def score(zz, largest):
            s = dot(query, ko[zz].reshape(span, HEAD_DIM), 1, 1) * score_scale
            scores[zz] = s
            return jnp.maximum(largest, jnp.max(s, axis=1, keepdims=True))

        largest = lax.fori_loop(0, z, score, jnp.max(own_scores, axis=1, keepdims=True))
        weights = jnp.exp(own_scores - largest)
        probs[z, h] = weights.astype(bf16)

        def weigh(zz, total):
            e = jnp.exp(scores[zz] - largest)
            probs[zz, h] = e.astype(bf16)
            return total + jnp.sum(e, axis=1, keepdims=True)

        total = lax.fori_loop(0, z, weigh, jnp.sum(weights, axis=1, keepdims=True))
        sums[h] = jnp.broadcast_to(total, (span, HEAD_DIM))

    def attend_some(j, first_j, n_js, here):
        heads_now = [h for h in range(q_heads) if first_j + h * n_js // q_heads == j]
        if heads_now:
            @pl.when(here)
            def _():
                if heads_now[0] == 0:
                    arrived(4)
                    for zz in range(nz - 1):
                        @pl.when(zz < z)
                        def _():
                            earlier(ko, zz, k_send, k_recv).wait_recv()
                for h in heads_now:
                    attend(h)

    def finish(i):
        @pl.when(z > 0)
        def _():
            chain(i).wait_recv()

            @pl.when(z < nz - 1)
            def _():
                sout[i] = before[n_blocks, i] * sin[i] + sout[i]
                chain(i).start()

        skip = jnp.where(
            left_half, skip_ref[0, p * heads + 2 * i], skip_ref[0, p * heads + 2 * i + 1]
        )
        for blk in range(n_blocks):
            mixes = []
            for h in (2 * i, 2 * i + 1):
                at = blk * heads + h
                gaps = jnp.where(causal, column(0, blk, h) - l_rows[at : at + 1, :], -jnp.inf)
                mixes.append((cross[blk] * jnp.exp(gaps) * steps[at : at + 1, :]).astype(bf16))
            xb = x_block(blk, i)
            both = dot(jnp.concatenate(mixes, axis=0), xb)
            local = jnp.where(left_half, both[:BLOCK], both[BLOCK:])
            dec, own = before[blk, i]
            state = dec * sin[i] + own
            high = state.astype(bf16)
            low = (state - high.astype(f32)).astype(bf16)
            carried = dot(c_blocks[blk], high) + dot(c_blocks[blk], low)
            y = local + grown[blk, i] * carried + skip * xb.astype(f32)
            yo[i, pl.ds(blk * per_block, per_block)] = y.astype(bf16).reshape(
                per_block, tok, BLOCK
            )
        for d in range(1, PLANE):
            give_back(i, d).start()
        yh[i, p] = yo[i, p]

    half = n_chunks // 2
    for i in range(n_chunks + 3):
        if i < n_chunks:
            summarize(i)
        j = i - 3
        if j >= 0:
            if j == 0:
                arrived(3)
                c_blocks = [
                    co[pl.ds(blk * per_block, per_block)].reshape(BLOCK, STATE)
                    for blk in range(n_blocks)
                ]
                cross = [dot(c_blocks[blk], b_blocks[blk], 1, 1) for blk in range(n_blocks)]
            finish(j)
            attend_some(j, 0, half, z == nz - 1)
            attend_some(j, half, half, z < nz - 1)

    load_z.wait()
    zg = z_ref[...].astype(f32)
    silu[...] = zg / (1.0 + jnp.exp(-zg))
    for i in range(n_chunks):
        for d in range(1, PLANE):
            give_back(i, d).wait_recv()
    group_lanes = chans // groups
    for g in range(groups):
        gc = slice(g * group_lanes, (g + 1) * group_lanes)
        owners = range(g * PLANE // groups, (g + 1) * PLANE // groups)
        ssm = jnp.concatenate([yh[i, j] for j in owners for i in range(n_chunks)], axis=1)
        gated = ssm.astype(f32) * silu[:, gc]
        inverse = lax.rsqrt(jnp.mean(gated * gated, axis=1, keepdims=True) + NORM_EPS)
        mo_ref[:, gc] = (gated * inverse * gain_ref[:, gc]).astype(bf16)

    store = pltpu.make_async_copy(mo_ref, mo_hbm, m_sem)
    store.start()

    def partial_copy(dt_, dp):
        tt, pp = (t + dt_) % n_tp, (p + dp) % PLANE
        return pltpu.make_async_remote_copy(
            src_ref=part.at[tt * kv_here + pp * kv_here // PLANE], dst_ref=vp.at[t, p],
            send_sem=p_send.at[dt_, dp], recv_sem=p_recv.at[dt_, dp],
            device_id=(seq_id(z, pp), tt), device_id_type=MESH,
        )

    offsets = [(dt_, dp) for dt_ in range(n_tp) for dp in range(PLANE) if dt_ or dp]
    load_w.wait()
    for n in range(w_ref.shape[1] // 256):
        product = dot(mo_ref[...], w_ref[:, n * 256 : (n + 1) * 256]).astype(bf16)
        part[2 * n] = product[:, :HEAD_DIM]
        part[2 * n + 1] = product[:, HEAD_DIM:]
        for dt_, dp in offsets:
            tt, pp = (t + dt_) % n_tp, (p + dp) % PLANE

            @pl.when((tt * kv_here + pp * kv_here // PLANE) // 2 == n)
            def _():
                partial_copy(dt_, dp).start()

    vp[t, p] = part[t * kv_here + p * kv_here // PLANE]
    accs[...] = jnp.zeros_like(accs)

    def take(zz):
        earlier(vo, zz, v_send, v_recv).wait_recv()
        for h in range(q_heads):
            accs[h] += dot(probs[zz, h], vo[zz].reshape(span, HEAD_DIM))

    for zz in range(nz - 2):
        @pl.when(zz < z - 1)
        def _():
            take(zz)

    for dt_, dp in offsets:
        partial_copy(dt_, dp).wait_recv()
    values = vp[0].astype(f32)
    for tt in range(1, n_tp):
        values = values + vp[tt].astype(f32)
    vo[z] = values.astype(bf16)
    push(vo, v_send, v_recv)

    for zz in range(nz - 1):
        @pl.when(zz == z - 1)
        def _():
            take(zz)

    def hand_out(h, d):
        return pltpu.make_async_remote_copy(
            src_ref=ao.at[h, (p + d) % PLANE], dst_ref=att_hbm.at[:, cols(p * q_heads + h, HEAD_DIM)],
            send_sem=o_send.at[h, d], recv_sem=o_recv.at[h, d],
            device_id=(seq_id(z, (p + d) % PLANE), t), device_id_type=MESH,
        )

    mine = []
    for h in range(q_heads):
        acc = accs[h] + dot(probs[z, h], vo[z].reshape(span, HEAD_DIM))
        ao[h] = (acc / sums[h]).astype(bf16).reshape(PLANE, tok, HEAD_DIM)
        for d in range(1, PLANE):
            hand_out(h, d).start()
        mine.append(
            pltpu.make_async_copy(
                ao.at[h, p], att_hbm.at[:, cols(p * q_heads + h, HEAD_DIM)], f_sem.at[h]
            )
        )
        mine[-1].start()

    for i in order:
        for d in range(1, PLANE):
            sends[i, d].wait_send()

    @pl.when(z < nz - 1)
    def _():
        for i in range(n_chunks):
            chain(i).wait_send()

    for i in range(n_chunks):
        for d in range(1, PLANE):
            give_back(i, d).wait_send()
    pushed(ko, k_send, k_recv)
    pushed(vo, v_send, v_recv)
    for dt_, dp in offsets:
        partial_copy(dt_, dp).wait_send()
    store.wait()
    for h in range(q_heads):
        mine[h].wait()
        for d in range(1, PLANE):
            hand_out(h, d).wait_recv()
            hand_out(h, d).wait_send()


def copy_out(mo_in, att_in, mo_out, att_out, mo_here, att_here, sem):
    loads = [
        pltpu.make_async_copy(mo_in, mo_here, sem.at[0]),
        pltpu.make_async_copy(att_in, att_here, sem.at[1]),
    ]
    stores = [
        pltpu.make_async_copy(mo_here, mo_out, sem.at[2]),
        pltpu.make_async_copy(att_here, att_out, sem.at[3]),
    ]
    for load in loads:
        load.start()
    for load, store in zip(loads, stores):
        load.wait()
        store.start()
    for store in stores:
        store.wait()


def per_device(
    n_seq, n_tp,
    mamba_x, gate_z, b_in, c_in, dt_raw, a_log, skip_d, norm_gain, value_weight, queries, keys,
):
    tok, chans = mamba_x.shape
    lanes = chans // PLANE
    heads = lanes // MHEAD_DIM
    nz = n_seq // PLANE
    span = PLANE * tok
    q_lanes = queries.shape[1] // PLANE
    q_heads = q_lanes // HEAD_DIM
    n_chunks = lanes // BLOCK
    n_blocks = span // BLOCK
    hbm = pl.BlockSpec(memory_space=pltpu.HBM)
    dma = pltpu.SemaphoreType.DMA
    results = pl.pallas_call(
        functools.partial(kernel, n_seq, n_tp),
        out_shape=(
            jax.ShapeDtypeStruct((tok, chans), bf16),
            jax.ShapeDtypeStruct(queries.shape, bf16),
        ),
        in_specs=[hbm] * 11,
        out_specs=(hbm, hbm),
        scratch_shapes=[
            pltpu.VMEM(value_weight.shape, bf16),
            pltpu.VMEM((tok, chans), bf16),
            pltpu.VMEM((n_chunks, PLANE, tok, BLOCK), bf16),
            pltpu.VMEM((PLANE, tok, STATE), bf16),
            pltpu.VMEM((PLANE, tok, STATE), bf16),
            pltpu.VMEM((PLANE, heads, tok), f32),
            pltpu.VMEM((PLANE, tok, q_lanes), bf16),
            pltpu.VMEM((nz, PLANE, tok, HEAD_DIM), bf16),
            pltpu.VMEM((nz, PLANE, tok, HEAD_DIM), bf16),
            pltpu.VMEM((n_chunks, STATE, BLOCK), f32),
            pltpu.VMEM((n_chunks, STATE, BLOCK), f32),
            pltpu.VMEM((n_chunks, PLANE, tok, BLOCK), bf16),
            pltpu.VMEM((n_chunks, PLANE, tok, BLOCK), bf16),
            pltpu.VMEM((KVHEADS, tok, HEAD_DIM), bf16),
            pltpu.VMEM((n_tp, PLANE, tok, HEAD_DIM), bf16),
            pltpu.VMEM((nz, span, span), f32),
            pltpu.VMEM((nz, q_heads, span, span), bf16),
            pltpu.VMEM((q_heads, span, HEAD_DIM), f32),
            pltpu.VMEM((q_heads, span, HEAD_DIM), f32),
            pltpu.VMEM((q_heads, PLANE, tok, HEAD_DIM), bf16),
            pltpu.VMEM((n_blocks, n_chunks, BLOCK, BLOCK), f32),
            pltpu.VMEM((tok, chans), f32),
            pltpu.VMEM((tok, chans), bf16),
            pltpu.SMEM((1, PLANE * heads), f32),
            pltpu.SMEM((1, PLANE * heads), f32),
            pltpu.VMEM((1, chans), f32),
            dma, dma, dma, dma((3,)), dma((5 + n_chunks,)),
            dma((5 + n_chunks, PLANE)), dma((5 + n_chunks, PLANE)),
            dma((nz,)), dma((nz,)),
            dma((n_chunks,)), dma((n_chunks,)),
            dma((n_chunks, PLANE)), dma((n_chunks, PLANE)),
            dma((n_tp, PLANE)), dma((n_tp, PLANE)),
            dma((nz,)), dma((nz,)),
            dma((q_heads, PLANE)), dma((q_heads, PLANE)), dma((q_heads,)),
        ],
        compiler_params=pltpu.CompilerParams(
            collective_id=0, has_side_effects=True, vmem_limit_bytes=62 * 1024 * 1024
        ),
    )(
        mamba_x, gate_z, b_in, c_in,
        dt_raw.reshape(PLANE, heads, tok), a_log.reshape(1, -1),
        skip_d.reshape(1, -1), norm_gain.reshape(1, chans), value_weight, queries, keys,
    )
    return pl.pallas_call(
        copy_out,
        out_shape=[jax.ShapeDtypeStruct(r.shape, r.dtype) for r in results],
        in_specs=[hbm] * 2,
        out_specs=[hbm] * 2,
        scratch_shapes=[pltpu.VMEM(r.shape, r.dtype) for r in results] + [dma((4,))],
        compiler_params=pltpu.CompilerParams(vmem_limit_bytes=62 * 1024 * 1024),
    )(*results)


def solution(mesh):
    placed = (
        P("seq", "tp"),
        P("seq", "tp"),
        P("seq", "tp"),
        P("seq", "tp"),
        P("tp", "seq"),
        P("tp"),
        P("tp"),
        P("tp"),
        P("tp", None),
        P("seq", "tp"),
        P("seq", "tp"),
    )
    return jax.shard_map(
        functools.partial(per_device, mesh.shape["seq"], mesh.shape["tp"]),
        mesh=mesh,
        in_specs=placed,
        out_specs=(P("seq", "tp"), P("seq", "tp")),
        check_vma=False,
    )
```
